768 devices in a mesh: fsdp: 12 (over z), grp: 64 (over y, x, core).
Axes of the slice: x: 4, y: 8, z: 12, core: 2. Of those that a mesh axis runs over, the one named last changes fastest.
Arguments:
- tokens: bfloat16 [98304, 4608], P(('fsdp', 'grp')), may hold values from -24 to 24
- w_values: bfloat16 [4608, 512], P(('fsdp', 'grp')), may hold values from -0.09375 to 0.09375
- w_scales: float32 [1152], replicated, may hold values from 0.25 to 4
- out_grad: bfloat16 [98304, 512], P(('fsdp', 'grp')), may hold values from -6 to 6
Outputs:
- projected: bfloat16 [98304, 512], P(('fsdp', 'grp'))
- token_grad: bfloat16 [98304, 4608], P(('fsdp', 'grp'))
- weight_grad: float32 [4608, 512], P(('fsdp', 'grp'))
The draws below stay inside these ranges and needn't reach their ends.
All inputs are finite; a program needn't handle non-finite values.
Results may differ from the reference program's by a relative error of at most 0.019.
Values may be sent and summed in bfloat16 or wider, within the bound.
No kernel may reach another device: no remote copies, remote signals or barrier semaphores. Data moves between devices by JAX's collectives and lax.ppermute only.
A program may use at most 64 MiB of HBM per device.

```python
import math
import jax
import jax.numpy as jnp
from jax import lax

D_WIN = 4608
KV_COLS = 512
BLOCK_ROWS = 4
TOK_DEV = 128
TOKENS = 98304
BLOCKS = 1152
N_FSDP = 12
N_GRP = 64


def strengthened(array, key, source, target, parts, factor):
    owner, partner = [(jnp.arange(array.shape[position]) // (array.shape[position] // parts)).reshape([-1 if axis == position else 1 for axis in range(array.ndim)]) for position in (source, target)]
    chosen = jax.random.permutation(key, parts)[partner]
    strong = (owner == chosen) | (owner == (partner + parts // 2) % parts)
    return jnp.where(strong, factor * array, array)


def shard_levels(stream_key, dims, shards, least, top_value):
    def one(axis_at, shards_of):
        heights = jax.random.uniform(jax.random.fold_in(jax.random.fold_in(stream_key, 6), axis_at), (shards_of,), jnp.float32, least / len(shards), top_value / len(shards))
        return jnp.repeat(jnp.exp(heights), dims[axis_at] // shards_of).reshape((-1,) + (1,) * (len(dims) - axis_at - 1))

    level = one(*shards[0])
    for cut in shards[1:]:
        level = level * one(*cut)
    return level


def noise(rng, shape, deviation, reach, cuts=(), held_as=jnp.bfloat16):
    loudness = shard_levels(rng, shape, cuts, -0.22, 0.18) if cuts else 1.0
    values = jax.random.normal(rng, shape, jnp.float32) * deviation * loudness
    return jnp.minimum(jnp.maximum(values, -reach), reach).astype(held_as)


def heavy_noise(stream_key, extent, scale, reach, pieces, heavy, kind=jnp.bfloat16):
    drawn = scale * jax.random.normal(stream_key, extent, jnp.float32)
    if pieces:
        drawn = drawn * shard_levels(stream_key, extent, pieces, -0.22, 0.18)
    return jnp.clip(strengthened(drawn, jax.random.fold_in(stream_key, 3), *heavy), -reach, reach).astype(kind)


def setup_inputs(seed: int = 0) -> dict:
    arg_keys = jax.random.split(jax.random.key(seed), 5)
    return {
        "tokens": heavy_noise(arg_keys[0], (TOKENS, D_WIN), 1.0, 24.0, ((0, 768),), (0, 1, 768, 6.0)),
        "w_values": noise(arg_keys[1], (D_WIN, KV_COLS), D_WIN ** -0.5, 0.09375, ((0, 768),)),
        "w_scales": jnp.clip(jnp.exp(jax.random.uniform(arg_keys[2], (BLOCKS,), jnp.float32, math.log(0.25), math.log(4.0))), 0.25, 4.0),
        "out_grad": noise(arg_keys[3], (TOKENS, KV_COLS), 1.0, 6.0, ((0, 768),)),
    }


def reference(tokens, w_values, w_scales, out_grad):
    row_scale = jnp.repeat(w_scales, BLOCK_ROWS)
    weights = (w_values.astype(jnp.float32) * row_scale[:, None]).astype(jnp.bfloat16)
    projected = jnp.dot(tokens, weights, preferred_element_type=jnp.float32).astype(jnp.bfloat16)
    token_grad = lax.dot_general(out_grad, weights, (((1,), (1,)), ((), ())), preferred_element_type=jnp.float32).astype(jnp.bfloat16)
    groups = N_FSDP * N_GRP
    token_groups = tokens.reshape(groups, TOK_DEV, D_WIN)
    grad_groups = out_grad.reshape(groups, TOK_DEV, KV_COLS)

    def accumulate(total, pair):
        partial_term = lax.dot_general(pair[0], pair[1], (((0,), (0,)), ((), ())), preferred_element_type=jnp.float32)
        return (total + partial_term.astype(jnp.bfloat16).astype(jnp.float32), None)
    total, unused = lax.scan(accumulate, jnp.zeros((D_WIN, KV_COLS), jnp.float32), (token_groups, grad_groups))
    weight_grad = total * (1.0 / math.sqrt(TOKENS))
    return (projected, token_grad, weight_grad)
```

```python
import math

import numpy as np
import jax
import jax.numpy as jnp
from jax import lax
from jax.sharding import Mesh, PartitionSpec as P

BLOCK_ROWS = 4
NZ, NY, NX, NC = 12, 8, 4, 2
AXES = ("z", "y", "x", "c")
BF16 = jnp.bfloat16
F32 = jnp.float32


def block_moves():
    moves = []
    for block in range(NZ * NY * NX * NC):
        rest, z = divmod(block, NZ)
        rest, y = divmod(rest, NY)
        c, x = divmod(rest, NX)
        moves.append((block, ((z * NY + y) * NX + x) * NC + c))
    return moves


def scaled_rows(w_values, w_scales):
    rows = w_values.shape[0]
    first = lax.axis_index(AXES) * rows
    start = first // BLOCK_ROWS
    pair = lax.dynamic_slice(w_scales, (start,), (2,))
    block = (first + lax.iota(jnp.int32, rows)) // BLOCK_ROWS - start
    scale = jnp.where(block == 0, pair[0], pair[1])
    return (w_values.astype(F32) * scale[:, None]).astype(BF16)


def gather(rows, axis, size):
    out = lax.all_to_all(jnp.broadcast_to(rows[None], (size, *rows.shape)), axis, 0, 0)
    return out.reshape(-1, rows.shape[1])


def reduce(rows, axis, size):
    out = lax.all_to_all(rows.reshape(size, -1, rows.shape[1]), axis, 0, 0)
    return jnp.sum(out.astype(F32), axis=0)


def body(tokens, w_values, w_scales, out_grad):
    moves = block_moves()
    rows = lax.ppermute(scaled_rows(w_values, w_scales), AXES, moves)
    partial = lax.dot_general(
        tokens, out_grad, (((0,), (0,)), ((), ())), preferred_element_type=F32
    ).astype(BF16)
    total = reduce(partial, "c", NC).astype(BF16)
    total = reduce(total, "x", NX).astype(BF16)
    total = reduce(total, "y", NY).astype(BF16)
    total = reduce(total, "z", NZ)
    count = tokens.shape[0] * NZ * NY * NX * NC
    weight_grad = lax.ppermute(
        total * (1.0 / math.sqrt(count)), AXES, [(b, a) for a, b in moves]
    )
    rows = gather(rows, "z", NZ)
    rows = gather(rows, "y", NY)
    rows = gather(rows, "x", NX)
    weights = gather(rows, "c", NC)
    projected = jnp.dot(tokens, weights, preferred_element_type=F32).astype(BF16)
    token_grad = lax.dot_general(
        out_grad, weights, (((1,), (1,)), ((), ())), preferred_element_type=F32
    ).astype(BF16)
    return projected, token_grad, weight_grad


def solution(mesh):
    split = Mesh(mesh.devices.reshape(NZ, NY, NX, NC), AXES)
    by_rows = P(AXES, None)
    return jax.shard_map(
        body,
        mesh=split,
        in_specs=(by_rows, by_rows, P(), by_rows),
        out_specs=(by_rows, by_rows, by_rows),
        check_vma=False,
    )
```

```python
import math

import jax
import jax.numpy as jnp
from jax import lax
from jax.sharding import Mesh, PartitionSpec as P

BLOCK_ROWS = 4
NZ, NY, NX, NC = 12, 8, 4, 2
AXES = ("z", "y", "x", "c")
BF16 = jnp.bfloat16
F32 = jnp.float32


def block_moves():
    moves = []
    for block in range(NZ * NY * NX * NC):
        rest, z = divmod(block, NZ)
        rest, y = divmod(rest, NY)
        c, x = divmod(rest, NX)
        moves.append((block, ((z * NY + y) * NX + x) * NC + c))
    return moves


def scaled_rows(w_values, w_scales):
    rows = w_values.shape[0]
    first = lax.axis_index(AXES) * rows
    start = first // BLOCK_ROWS
    pair = lax.dynamic_slice(w_scales, (start,), (2,))
    block = (first + lax.iota(jnp.int32, rows)) // BLOCK_ROWS - start
    scale = jnp.where(block == 0, pair[0], pair[1])
    return (w_values.astype(F32) * scale[:, None]).astype(BF16)


def gather(rows, axis, size):
    out = lax.all_to_all(jnp.broadcast_to(rows[None], (size, *rows.shape)), axis, 0, 0)
    return out.reshape(-1, rows.shape[1])


def reduce(rows, axis, size):
    out = lax.all_to_all(rows.reshape(size, -1, rows.shape[1]), axis, 0, 0)
    return jnp.sum(out.astype(F32), axis=0)


def swap(array):
    return lax.ppermute(array, "c", [(0, 1), (1, 0)])


def dot(a, b, over):
    return lax.dot_general(a, b, ((over[:1], over[1:]), ((), ())), preferred_element_type=F32)


def body(tokens, w_values, w_scales, out_grad):
    moves = block_moves()
    core = lax.axis_index("c")
    half = tokens.shape[1] // NC
    low, high = tokens[:, :half], tokens[:, half:]
    mine = jnp.where(core == 0, low, high)
    theirs = swap(jnp.where(core == 0, high, low))
    their_grad = swap(out_grad)
    rows = lax.ppermute(scaled_rows(w_values, w_scales), AXES, moves)

    partial = (dot(mine, out_grad, (0, 0)) + dot(theirs, their_grad, (0, 0))).astype(BF16)
    partial, rows = lax.optimization_barrier((partial, rows))
    total = lax.psum_scatter(partial, "x", scatter_dimension=0, tiled=True)
    total = reduce(total, "y", NY).astype(BF16)
    total = reduce(total, "z", NZ)

    rows = gather(rows, "z", NZ)
    rows = gather(rows, "y", NY)
    weights = lax.all_gather(rows, "x", axis=0, tiled=True)
    total, weights = lax.optimization_barrier((total, weights))
    count = tokens.shape[0] * NZ * NY * NX * NC
    weight_grad = lax.ppermute(
        total * (1.0 / math.sqrt(count)), AXES, [(b, a) for a, b in moves]
    )
    for_them = swap(dot(theirs, weights, (1, 0)))
    grad_for_them = swap(dot(their_grad, weights, (1, 1)).astype(BF16))
    projected = (dot(mine, weights, (1, 0)) + for_them).astype(BF16)
    grad = dot(out_grad, weights, (1, 1)).astype(BF16)
    token_grad = jnp.concatenate(
        [jnp.where(core == 0, grad, grad_for_them), jnp.where(core == 0, grad_for_them, grad)],
        axis=1,
    )
    return projected, token_grad, weight_grad


def solution(mesh):
    split = Mesh(mesh.devices.reshape(NZ, NY, NX, NC), AXES)
    by_rows = P(AXES, None)
    return jax.shard_map(
        body,
        mesh=split,
        in_specs=(by_rows, by_rows, P(), by_rows),
        out_specs=(by_rows, by_rows, by_rows),
        check_vma=False,
    )
```

```python
import math

import jax
import jax.numpy as jnp
from jax import lax
from jax.experimental import pallas as pl
from jax.experimental.pallas import tpu as pltpu
from jax.sharding import Mesh, PartitionSpec as P

BLOCK_ROWS = 4
NZ, NY, NX, NC = 12, 8, 4, 2
AXES = ("z", "y", "x", "c")
BF16 = jnp.bfloat16
F32 = jnp.float32
PARAMS = pltpu.CompilerParams(vmem_limit_bytes=40 * 2**20)


def block_moves():
    moves = []
    for block in range(NZ * NY * NX * NC):
        rest, z = divmod(block, NZ)
        rest, y = divmod(rest, NY)
        c, x = divmod(rest, NX)
        moves.append((block, ((z * NY + y) * NX + x) * NC + c))
    return moves


def scaled_rows(w_values, w_scales):
    rows = w_values.shape[0]
    first = lax.axis_index(AXES) * rows
    start = first // BLOCK_ROWS
    pair = lax.dynamic_slice(w_scales, (start,), (2,))
    block = (first + lax.iota(jnp.int32, rows)) // BLOCK_ROWS - start
    scale = jnp.where(block == 0, pair[0], pair[1])
    return (w_values.astype(F32) * scale[:, None]).astype(BF16)


def swap(array):
    return lax.ppermute(array, "c", [(0, 1), (1, 0)])


def along_x(array, step):
    return lax.ppermute(array, "x", [(i, (i + step) % NX) for i in range(NX)])


def dot(a, b, over):
    return lax.dot_general(a, b, ((over[:1], over[1:]), ((), ())), preferred_element_type=F32)


def whole(shape):
    return pl.BlockSpec(shape, lambda i, place: (0,) * len(shape))


def call(kernel, outs, in_specs, scratch, flops, args):
    moved = sum(math.prod(s.shape) * s.dtype.itemsize for s in outs)
    return pl.pallas_call(
        kernel,
        out_shape=outs,
        grid_spec=pltpu.PrefetchScalarGridSpec(
            num_scalar_prefetch=1,
            grid=(1,),
            in_specs=in_specs,
            out_specs=[whole(s.shape) for s in outs],
            scratch_shapes=scratch,
        ),
        compiler_params=PARAMS,
        cost_estimate=pl.CostEstimate(flops=flops, bytes_accessed=2 * moved, transcendentals=0),
    )(*args)


def partials(place, tokens, grad, theirs):
    count, half = tokens.shape[0], tokens.shape[1] // NC
    cols = grad.shape[1]
    rows = half // NX
    chunk = 256

    def kernel(place_ref, tokens_ref, grad_ref, theirs_ref, *rest):
        outs, total = rest[:NX], rest[NX]
        grads = jnp.concatenate([grad_ref[...], theirs_ref[:, half:]], axis=0)
        for k in range(0, half, chunk):
            both = jnp.concatenate(
                [tokens_ref[:, k : k + chunk], theirs_ref[:, k : k + chunk]], axis=0
            )
            total[k : k + chunk] = dot(both, grads, (0, 0)).astype(BF16)
        x = place_ref[1]
        for step in range(NX):
            block = lax.rem(x + step, NX)
            outs[step][...] = total[pl.ds(pl.multiple_of(block * rows, rows), rows), :]

    return call(
        kernel,
        [jax.ShapeDtypeStruct((rows, cols), BF16)] * NX,
        [
            pl.BlockSpec((count, half), lambda i, place: (0, place[0])),
            whole(grad.shape),
            whole(theirs.shape),
        ],
        [pltpu.VMEM((half, cols), BF16)],
        4 * count * half * cols,
        (place, tokens, grad, theirs),
    )


def forward(place, tokens, grad, blocks, theirs=None):
    own = theirs is None
    half = blocks[0].shape[0] * NX
    rows, cols = blocks[0].shape
    count = tokens.shape[0] if own else theirs.shape[0]

    def kernel(place_ref, *refs):
        if own:
            tokens_ref, grad_ref, *block_refs, part_ref, out_ref, weights = refs
            token, gradient = tokens_ref[...], grad_ref[...]
        else:
            theirs_ref, *block_refs, out_ref, weights = refs
            token, gradient = theirs_ref[:, :half], theirs_ref[:, half:]
        x = place_ref[1]
        for step in range(NX):
            block = lax.rem(x + NX - step, NX)
            weights[pl.ds(pl.multiple_of(block * rows, rows), rows), :] = block_refs[step][...]
        part = dot(token, weights[...], (1, 0))
        columns = dot(gradient, weights[...], (1, 1)).astype(BF16)
        out_ref[:, :half] = columns
        if own:
            part_ref[...] = part
        else:
            out_ref[:, half:] = part.astype(BF16)

    block_specs = [whole(b.shape) for b in blocks]
    if own:
        outs = [
            jax.ShapeDtypeStruct((count, cols), F32),
            jax.ShapeDtypeStruct((count, half), BF16),
        ]
        specs = [
            pl.BlockSpec((count, half), lambda i, place: (0, place[0])),
            whole(grad.shape),
            *block_specs,
        ]
        args = (place, tokens, grad, *blocks)
    else:
        outs = [jax.ShapeDtypeStruct((count, half + cols), BF16)]
        specs = [whole(theirs.shape), *block_specs]
        args = (place, theirs, *blocks)
    return call(
        kernel, outs, specs, [pltpu.VMEM((half, cols), BF16)], 4 * count * half * cols, args
    )


def assemble(place, part, columns, received):
    count, half = columns.shape
    cols = part.shape[1]

    def kernel(place_ref, part_ref, columns_ref, received_ref, projected_ref, out_ref):
        projected_ref[...] = (part_ref[...] + received_ref[:, half:].astype(F32)).astype(BF16)
        core = place_ref[0]

        @pl.when(core == 0)
        def _():
            out_ref[:, :half] = columns_ref[...]
            out_ref[:, half:] = received_ref[:, :half]

        @pl.when(core == 1)
        def _():
            out_ref[:, :half] = received_ref[:, :half]
            out_ref[:, half:] = columns_ref[...]

    return call(
        kernel,
        [
            jax.ShapeDtypeStruct((count, cols), BF16),
            jax.ShapeDtypeStruct((count, NC * half), BF16),
        ],
        [whole(part.shape), whole(columns.shape), whole(received.shape)],
        [],
        count * cols,
        (place, part, columns, received),
    )


def body(tokens, w_values, w_scales, out_grad):
    moves = block_moves()
    core, x = lax.axis_index("c"), lax.axis_index("x")
    place = jnp.stack([core, x]).astype(jnp.int32)
    half = tokens.shape[1] // NC
    cols = out_grad.shape[1]
    others = lax.dynamic_slice(tokens, (0, (1 - core) * half), (tokens.shape[0], half))
    theirs = swap(jnp.concatenate([others, out_grad], axis=1))
    rows = lax.ppermute(scaled_rows(w_values, w_scales), AXES, moves)

    parts = partials(place, tokens, out_grad, theirs)
    rows, *parts = lax.optimization_barrier((rows, *parts))
    parts = [parts[0], *(along_x(parts[step], step) for step in range(1, NX))]

    rows = lax.all_to_all(jnp.broadcast_to(rows[None], (NZ, *rows.shape)), "z", 0, 0)
    rows = rows.reshape(-1, cols)
    total = sum(p.astype(F32) for p in parts).astype(BF16)
    both = jnp.concatenate(
        [
            total.reshape(NY, -1, cols),
            jnp.broadcast_to(rows[None], (NY, *rows.shape)),
        ],
        axis=1,
    )
    both = lax.all_to_all(both, "y", 0, 0)
    share = both.shape[1] // 2
    rows = both[:, share:].reshape(-1, cols)
    blocks = [rows, *(along_x(rows, step) for step in range(1, NX))]

    total = jnp.sum(both[:, :share].astype(F32), axis=0).astype(BF16)
    total = lax.all_to_all(total.reshape(NZ, -1, cols), "z", 0, 0)
    total = jnp.sum(total.astype(F32), axis=0)
    total, *blocks = lax.optimization_barrier((total, *blocks))
    count = tokens.shape[0] * NZ * NY * NX * NC
    weight_grad = lax.ppermute(
        total * (1.0 / math.sqrt(count)), AXES, [(b, a) for a, b in moves]
    )

    (for_them,) = forward(place, None, None, blocks, theirs)
    received = swap(for_them)
    part, columns = forward(place, tokens, out_grad, blocks)
    projected, token_grad = assemble(place, part, columns, received)
    return projected, token_grad, weight_grad


def solution(mesh):
    split = Mesh(mesh.devices.reshape(NZ, NY, NX, NC), AXES)
    by_rows = P(AXES, None)
    return jax.shard_map(
        body,
        mesh=split,
        in_specs=(by_rows, by_rows, P(), by_rows),
        out_specs=(by_rows, by_rows, by_rows),
        check_vma=False,
    )
```

```python
import math

import jax
import jax.numpy as jnp
from jax import lax
from jax.experimental import pallas as pl
from jax.experimental.pallas import tpu as pltpu
from jax.sharding import Mesh, PartitionSpec as P

BLOCK_ROWS = 4
NZ, NY, NX, NC = 12, 8, 4, 2
AXES = ("z", "y", "x", "c")
PLANE = ("z", "y")
BF16 = jnp.bfloat16
F32 = jnp.float32
PARAMS = pltpu.CompilerParams(vmem_limit_bytes=40 * 2**20)


def block_moves():
    moves = []
    for block in range(NZ * NY * NX * NC):
        rest, y = divmod(block, NY)
        rest, z = divmod(rest, NZ)
        c, x = divmod(rest, NX)
        moves.append((block, ((z * NY + y) * NX + x) * NC + c))
    return moves


def scaled_rows(w_values, w_scales):
    rows = w_values.shape[0]
    first = lax.axis_index(AXES) * rows
    start = first // BLOCK_ROWS
    pair = lax.dynamic_slice(w_scales, (start,), (2,))
    block = (first + lax.iota(jnp.int32, rows)) // BLOCK_ROWS - start
    scale = jnp.where(block == 0, pair[0], pair[1])
    return (w_values.astype(F32) * scale[:, None]).astype(BF16)


def swap(array):
    return lax.ppermute(array, "c", [(0, 1), (1, 0)])


def along_x(array, step):
    return lax.ppermute(array, "x", [(i, (i + step) % NX) for i in range(NX)])


def dot(a, b, over):
    return lax.dot_general(a, b, ((over[:1], over[1:]), ((), ())), preferred_element_type=F32)


def call(kernel, outs, scratch, flops, place, *args):
    moved = sum(math.prod(s.shape) * s.dtype.itemsize for s in outs)
    vmem = pl.BlockSpec(memory_space=pltpu.VMEM)
    return pl.pallas_call(
        kernel,
        out_shape=outs,
        in_specs=[pl.BlockSpec(memory_space=pltpu.SMEM), *[vmem] * len(args)],
        out_specs=[vmem] * len(outs),
        scratch_shapes=scratch,
        compiler_params=PARAMS,
        cost_estimate=pl.CostEstimate(flops=flops, bytes_accessed=2 * moved, transcendentals=0),
    )(place, *args)


def core_columns(place_ref, half):
    return pl.multiple_of(place_ref[0] * half, half)


def partials(place, tokens, grad, theirs):
    count, half = tokens.shape[0], tokens.shape[1] // NC
    cols = grad.shape[1]
    rows = half // NX
    chunk = 256

    def kernel(place_ref, tokens_ref, grad_ref, theirs_ref, *rest):
        outs, total = rest[:NX], rest[NX]
        grads = jnp.concatenate([grad_ref[...], theirs_ref[:, half:]], axis=0)
        first = core_columns(place_ref, half)
        for k in range(0, half, chunk):
            mine = tokens_ref[:, pl.ds(pl.multiple_of(first + k, chunk), chunk)]
            both = jnp.concatenate([mine, theirs_ref[:, k : k + chunk]], axis=0)
            total[k : k + chunk] = dot(both, grads, (0, 0)).astype(BF16)
        x = place_ref[1]
        for step in range(NX):
            block = lax.rem(x + step, NX)
            outs[step][...] = total[pl.ds(pl.multiple_of(block * rows, rows), rows), :]

    return call(
        kernel,
        [jax.ShapeDtypeStruct((rows, cols), BF16)] * NX,
        [pltpu.VMEM((half, cols), BF16)],
        4 * count * half * cols,
        place,
        tokens,
        grad,
        theirs,
    )


def forward(place, tokens, grad, blocks, theirs=None):
    own = theirs is None
    half = blocks[0].shape[0] * NX
    rows, cols = blocks[0].shape
    count = tokens.shape[0] if own else theirs.shape[0]

    def kernel(place_ref, *refs):
        if own:
            tokens_ref, grad_ref, *block_refs, part_ref, out_ref, weights = refs
            token = tokens_ref[:, pl.ds(core_columns(place_ref, half), half)]
            gradient = grad_ref[...]
        else:
            theirs_ref, *block_refs, out_ref, weights = refs
            token, gradient = theirs_ref[:, :half], theirs_ref[:, half:]
        x = place_ref[1]
        for step in range(NX):
            block = lax.rem(x + NX - step, NX)
            weights[pl.ds(pl.multiple_of(block * rows, rows), rows), :] = block_refs[step][...]
        part = dot(token, weights[...], (1, 0))
        columns = dot(gradient, weights[...], (1, 1)).astype(BF16)
        out_ref[:, :half] = columns
        if own:
            part_ref[...] = part
        else:
            out_ref[:, half:] = part.astype(BF16)

    if own:
        outs = [
            jax.ShapeDtypeStruct((count, cols), F32),
            jax.ShapeDtypeStruct((count, half), BF16),
        ]
        args = (tokens, grad, *blocks)
    else:
        outs = [jax.ShapeDtypeStruct((count, half + cols), BF16)]
        args = (theirs, *blocks)
    return call(
        kernel, outs, [pltpu.VMEM((half, cols), BF16)], 4 * count * half * cols, place, *args
    )


def assemble(place, part, columns, received):
    count, half = columns.shape
    cols = part.shape[1]

    def kernel(place_ref, part_ref, columns_ref, received_ref, projected_ref, out_ref):
        projected_ref[...] = (part_ref[...] + received_ref[:, half:].astype(F32)).astype(BF16)
        core = place_ref[0]

        @pl.when(core == 0)
        def _():
            out_ref[:, :half] = columns_ref[...]
            out_ref[:, half:] = received_ref[:, :half]

        @pl.when(core == 1)
        def _():
            out_ref[:, :half] = received_ref[:, :half]
            out_ref[:, half:] = columns_ref[...]

    return call(
        kernel,
        [
            jax.ShapeDtypeStruct((count, cols), BF16),
            jax.ShapeDtypeStruct((count, NC * half), BF16),
        ],
        [],
        count * cols,
        place,
        part,
        columns,
        received,
    )


def body(tokens, w_values, w_scales, out_grad):
    moves = block_moves()
    core, x = lax.axis_index("c"), lax.axis_index("x")
    place = jnp.stack([core, x]).astype(jnp.int32)
    half = tokens.shape[1] // NC
    cols = out_grad.shape[1]
    others = lax.dynamic_slice(tokens, (0, (1 - core) * half), (tokens.shape[0], half))
    theirs = swap(jnp.concatenate([others, out_grad], axis=1))
    rows = lax.ppermute(scaled_rows(w_values, w_scales), AXES, moves)

    parts = partials(place, tokens, out_grad, theirs)
    rows, *parts = lax.optimization_barrier((rows, *parts))
    parts = [parts[0], *(along_x(parts[step], step) for step in range(1, NX))]

    rows = lax.all_to_all(jnp.broadcast_to(rows[None], (NZ * NY, *rows.shape)), PLANE, 0, 0)
    rows = rows.reshape(-1, cols)
    total = sum(p.astype(F32) for p in parts).astype(BF16)
    total, rows = lax.optimization_barrier((total, rows))
    blocks = [rows, *(along_x(rows, step) for step in range(1, NX))]
    total = lax.all_to_all(total.reshape(NZ * NY, -1, cols), PLANE, 0, 0)
    total = jnp.sum(total.astype(F32), axis=0)
    total, *blocks = lax.optimization_barrier((total, *blocks))
    count = tokens.shape[0] * NZ * NY * NX * NC
    weight_grad = lax.ppermute(
        total * (1.0 / math.sqrt(count)), AXES, [(b, a) for a, b in moves]
    )

    (for_them,) = forward(place, None, None, blocks, theirs)
    received = swap(for_them)
    part, columns = forward(place, tokens, out_grad, blocks)
    projected, token_grad = assemble(place, part, columns, received)
    return projected, token_grad, weight_grad


def solution(mesh):
    split = Mesh(mesh.devices.reshape(NZ, NY, NX, NC), AXES)
    by_rows = P(AXES, None)
    return jax.shard_map(
        body,
        mesh=split,
        in_specs=(by_rows, by_rows, P(), by_rows),
        out_specs=(by_rows, by_rows, by_rows),
        check_vma=False,
    )
```

```python
import math

import jax
import jax.numpy as jnp
from jax import lax
from jax.experimental import pallas as pl
from jax.experimental.pallas import tpu as pltpu
from jax.sharding import Mesh, PartitionSpec as P

BLOCK_ROWS = 4
NZ, NY, NX, NC = 12, 8, 4, 2
AXES = ("z", "y", "x", "c")
PLANE = ("z", "y")
BF16 = jnp.bfloat16
F32 = jnp.float32
LONG = 10**11
PARAMS = pltpu.CompilerParams(vmem_limit_bytes=16 * 2**20)


def block_moves():
    moves = []
    for block in range(NZ * NY * NX * NC):
        rest, y = divmod(block, NY)
        rest, z = divmod(rest, NZ)
        c, x = divmod(rest, NX)
        moves.append((block, ((z * NY + y) * NX + x) * NC + c))
    return moves


def scaled_rows(w_values, w_scales):
    rows = w_values.shape[0]
    first = lax.axis_index(AXES) * rows
    start = first // BLOCK_ROWS
    pair = lax.dynamic_slice(w_scales, (start,), (2,))
    block = (first + lax.iota(jnp.int32, rows)) // BLOCK_ROWS - start
    scale = jnp.where(block == 0, pair[0], pair[1])
    return (w_values.astype(F32) * scale[:, None]).astype(BF16)


def swap(array):
    return lax.ppermute(array, "c", [(0, 1), (1, 0)])


def along_x(array, step):
    return lax.ppermute(array, "x", [(i, (i + step) % NX) for i in range(NX)])


def dot(a, b, over):
    return lax.dot_general(a, b, ((over[:1], over[1:]), ((), ())), preferred_element_type=F32)


def call(kernel, outs, scratch, flops, place, *args):
    moved = sum(math.prod(s.shape) * s.dtype.itemsize for s in outs)
    vmem = pl.BlockSpec(memory_space=pltpu.VMEM)
    return pl.pallas_call(
        kernel,
        out_shape=outs,
        in_specs=[pl.BlockSpec(memory_space=pltpu.SMEM), *[vmem] * len(args)],
        out_specs=[vmem] * len(outs),
        scratch_shapes=scratch,
        compiler_params=PARAMS,
        cost_estimate=pl.CostEstimate(flops=flops, bytes_accessed=2 * moved, transcendentals=0),
    )(place, *args)


def core_columns(place_ref, half):
    return pl.multiple_of(place_ref[0] * half, half)


def partials(place, tokens, grad, theirs):
    count, half = tokens.shape[0], tokens.shape[1] // NC
    cols = grad.shape[1]
    rows = half // NX
    chunk = 256

    def kernel(place_ref, tokens_ref, grad_ref, theirs_ref, *rest):
        outs, total = rest[:NX], rest[NX]
        grads = jnp.concatenate([grad_ref[...], theirs_ref[:, half:]], axis=0)
        first = core_columns(place_ref, half)
        for k in range(0, half, chunk):
            mine = tokens_ref[:, pl.ds(pl.multiple_of(first + k, chunk), chunk)]
            both = jnp.concatenate([mine, theirs_ref[:, k : k + chunk]], axis=0)
            total[k : k + chunk] = dot(both, grads, (0, 0)).astype(BF16)
        x = place_ref[1]
        for step in range(NX):
            block = lax.rem(x + step, NX)
            outs[step][...] = total[pl.ds(pl.multiple_of(block * rows, rows), rows), :]

    return call(
        kernel,
        [jax.ShapeDtypeStruct((rows, cols), BF16)] * NX,
        [pltpu.VMEM((half, cols), BF16)],
        4 * count * half * cols,
        place,
        tokens,
        grad,
        theirs,
    )


def forward(place, tokens, grad, theirs, blocks):
    rows, cols = blocks[0].shape
    half = rows * NX
    count = tokens.shape[0]

    def kernel(place_ref, tokens_ref, grad_ref, theirs_ref, *rest):
        block_refs, (for_them, part_ref, columns_ref, weights) = rest[:NX], rest[NX:]
        x = place_ref[1]
        for step in range(NX):
            block = lax.rem(x + NX - step, NX)
            weights[pl.ds(pl.multiple_of(block * rows, rows), rows), :] = block_refs[step][...]
        mine = tokens_ref[:, pl.ds(core_columns(place_ref, half), half)]
        tokens_both = jnp.concatenate([theirs_ref[:, :half], mine], axis=0)
        part = dot(tokens_both, weights[...], (1, 0))
        for_them[:, half:] = part[:count].astype(BF16)
        part_ref[...] = part[count:]
        grads = jnp.concatenate([theirs_ref[:, half:], grad_ref[...]], axis=0)
        columns = dot(grads, weights[...], (1, 1)).astype(BF16)
        for_them[:, :half] = columns[:count]
        columns_ref[...] = columns[count:]

    return call(
        kernel,
        [
            jax.ShapeDtypeStruct((count, half + cols), BF16),
            jax.ShapeDtypeStruct((count, cols), F32),
            jax.ShapeDtypeStruct((count, half), BF16),
        ],
        [pltpu.VMEM((half, cols), BF16)],
        LONG,
        place,
        tokens,
        grad,
        theirs,
        *blocks,
    )


def add_up(place, parts):
    def kernel(place_ref, *refs):
        *part_refs, out_ref = refs
        out_ref[...] = sum(p[...].astype(F32) for p in part_refs).astype(BF16)

    out = jax.ShapeDtypeStruct(parts[0].shape, BF16)
    return call(kernel, [out], [], LONG, place, *parts)[0]


def assemble(place, part, columns, received):
    count, half = columns.shape
    cols = part.shape[1]

    def kernel(place_ref, part_ref, columns_ref, received_ref, projected_ref, out_ref):
        projected_ref[...] = (part_ref[...] + received_ref[:, half:].astype(F32)).astype(BF16)
        core = place_ref[0]

        @pl.when(core == 0)
        def _():
            out_ref[:, :half] = columns_ref[...]
            out_ref[:, half:] = received_ref[:, :half]

        @pl.when(core == 1)
        def _():
            out_ref[:, :half] = received_ref[:, :half]
            out_ref[:, half:] = columns_ref[...]

    return call(
        kernel,
        [
            jax.ShapeDtypeStruct((count, cols), BF16),
            jax.ShapeDtypeStruct((count, NC * half), BF16),
        ],
        [],
        count * cols,
        place,
        part,
        columns,
        received,
    )


def body(tokens, w_values, w_scales, out_grad):
    moves = block_moves()
    core, x = lax.axis_index("c"), lax.axis_index("x")
    place = jnp.stack([core, x]).astype(jnp.int32)
    half = tokens.shape[1] // NC
    cols = out_grad.shape[1]
    others = lax.dynamic_slice(tokens, (0, (1 - core) * half), (tokens.shape[0], half))
    theirs = swap(jnp.concatenate([others, out_grad], axis=1))
    rows = scaled_rows(w_values, w_scales)

    parts = partials(place, tokens, out_grad, theirs)
    rows, *parts = lax.optimization_barrier((rows, *parts))
    rows = lax.ppermute(rows, AXES, moves)
    parts = [parts[0], *(along_x(parts[step], step) for step in range(1, NX))]

    rows = lax.all_to_all(jnp.broadcast_to(rows[None], (NZ * NY, *rows.shape)), PLANE, 0, 0)
    rows = rows.reshape(-1, cols)
    total = add_up(place, parts)
    total, rows = lax.optimization_barrier((total, rows))
    blocks = [rows, *(along_x(rows, step) for step in range(1, NX))]
    total = lax.all_to_all(total.reshape(NZ * NY, -1, cols), PLANE, 0, 0)
    total = jnp.sum(total.astype(F32), axis=0)
    count = tokens.shape[0] * NZ * NY * NX * NC
    weight_grad = lax.ppermute(
        total * (1.0 / math.sqrt(count)), AXES, [(b, a) for a, b in moves]
    )

    for_them, part, columns = forward(place, tokens, out_grad, theirs, blocks)
    received = swap(for_them)
    projected, token_grad = assemble(place, part, columns, received)
    return projected, token_grad, weight_grad


def solution(mesh):
    split = Mesh(mesh.devices.reshape(NZ, NY, NX, NC), AXES)
    by_rows = P(AXES, None)
    return jax.shard_map(
        body,
        mesh=split,
        in_specs=(by_rows, by_rows, P(), by_rows),
        out_specs=(by_rows, by_rows, by_rows),
        check_vma=False,
    )
```

```python
import math

import numpy as np
import jax
import jax.numpy as jnp
from jax import lax
from jax.experimental import pallas as pl
from jax.experimental.pallas import tpu as pltpu
from jax.sharding import Mesh, PartitionSpec as P

BLOCK_ROWS = 4
AXES = {"z_far": 6, "z_near": 2, "y_far": 4, "y_near": 2, "x": 4, "c": 2}
NEAR, FAR = ("z_near", "y_near", "x"), ("z_far", "y_far")
NC = AXES["c"]


def devices(axes):
    return math.prod(AXES[a] for a in axes)


BF16 = jnp.bfloat16
F32 = jnp.float32
PARAMS = pltpu.CompilerParams(vmem_limit_bytes=16 * 2**20)


def block_moves():
    names = list(AXES)
    order = [names.index(a) for a in ("c", *NEAR, *FAR)]
    holders = np.arange(devices(names)).reshape(list(AXES.values())).transpose(order).reshape(-1)
    return [(block, int(holder)) for block, holder in enumerate(holders)]


def scaled_rows(w_values, w_scales):
    rows = w_values.shape[0]
    first = lax.axis_index(tuple(AXES)) * rows
    start = first // BLOCK_ROWS
    pair = lax.dynamic_slice(w_scales, (start,), (2,))
    block = (first + lax.iota(jnp.int32, rows)) // BLOCK_ROWS - start
    scale = jnp.where(block == 0, pair[0], pair[1])
    return (w_values.astype(F32) * scale[:, None]).astype(BF16)


def swap(array):
    return lax.ppermute(array, "c", [(0, 1), (1, 0)])


def gather(rows, axes):
    size = devices(axes)
    out = lax.all_to_all(jnp.broadcast_to(rows[None], (size, *rows.shape)), axes, 0, 0)
    return out.reshape(-1, rows.shape[1])


def reduce(rows, axes):
    out = lax.all_to_all(rows.reshape(devices(axes), -1, rows.shape[1]), axes, 0, 0)
    return jnp.sum(out.astype(F32), axis=0)


def dot(a, b, over):
    return lax.dot_general(a, b, ((over[:1], over[1:]), ((), ())), preferred_element_type=F32)


def call(kernel, outs, flops, place, *args):
    moved = sum(math.prod(s.shape) * s.dtype.itemsize for s in outs)
    vmem = pl.BlockSpec(memory_space=pltpu.VMEM)
    return pl.pallas_call(
        kernel,
        out_shape=outs,
        in_specs=[pl.BlockSpec(memory_space=pltpu.SMEM), *[vmem] * len(args)],
        out_specs=[vmem] * len(outs),
        compiler_params=PARAMS,
        cost_estimate=pl.CostEstimate(flops=flops, bytes_accessed=2 * moved, transcendentals=0),
    )(place, *args)


def core_columns(place_ref, half):
    return pl.multiple_of(place_ref[0] * half, half)


def partials(place, tokens, grad, theirs):
    half, cols = tokens.shape[1] // NC, grad.shape[1]
    chunk = 256

    def kernel(place_ref, tokens_ref, grad_ref, theirs_ref, out_ref):
        grads = jnp.concatenate([grad_ref[...], theirs_ref[:, half:]], axis=0)
        first = core_columns(place_ref, half)
        for k in range(0, half, chunk):
            mine = tokens_ref[:, pl.ds(pl.multiple_of(first + k, chunk), chunk)]
            both = jnp.concatenate([mine, theirs_ref[:, k : k + chunk]], axis=0)
            out_ref[k : k + chunk] = dot(both, grads, (0, 0)).astype(BF16)

    out = jax.ShapeDtypeStruct((half, cols), BF16)
    return call(kernel, [out], 4 * tokens.size * cols // NC, place, tokens, grad, theirs)[0]


def forward(place, tokens, grad, theirs, weights):
    half, cols = weights.shape
    count = tokens.shape[0]

    def kernel(place_ref, tokens_ref, grad_ref, theirs_ref, weights_ref, *outs):
        for_them, part_ref, columns_ref = outs
        mine = tokens_ref[:, pl.ds(core_columns(place_ref, half), half)]
        tokens_both = jnp.concatenate([theirs_ref[:, :half], mine], axis=0)
        part = dot(tokens_both, weights_ref[...], (1, 0))
        for_them[:, half:] = part[:count].astype(BF16)
        part_ref[...] = part[count:]
        grads = jnp.concatenate([theirs_ref[:, half:], grad_ref[...]], axis=0)
        columns = dot(grads, weights_ref[...], (1, 1)).astype(BF16)
        for_them[:, :half] = columns[:count]
        columns_ref[...] = columns[count:]

    outs = [
        jax.ShapeDtypeStruct((count, half + cols), BF16),
        jax.ShapeDtypeStruct((count, cols), F32),
        jax.ShapeDtypeStruct((count, half), BF16),
    ]
    return call(kernel, outs, 8 * count * half * cols, place, tokens, grad, theirs, weights)


def assemble(place, part, columns, received):
    count, half = columns.shape
    cols = part.shape[1]

    def kernel(place_ref, part_ref, columns_ref, received_ref, projected_ref, out_ref):
        projected_ref[...] = (part_ref[...] + received_ref[:, half:].astype(F32)).astype(BF16)
        core = place_ref[0]

        @pl.when(core == 0)
        def _():
            out_ref[:, :half] = columns_ref[...]
            out_ref[:, half:] = received_ref[:, :half]

        @pl.when(core == 1)
        def _():
            out_ref[:, :half] = received_ref[:, :half]
            out_ref[:, half:] = columns_ref[...]

    return call(
        kernel,
        [
            jax.ShapeDtypeStruct((count, cols), BF16),
            jax.ShapeDtypeStruct((count, NC * half), BF16),
        ],
        count * cols,
        place,
        part,
        columns,
        received,
    )


def body(tokens, w_values, w_scales, out_grad):
    moves = block_moves()
    core = lax.axis_index("c")
    place = core.astype(jnp.int32).reshape(1)
    count, half = tokens.shape[0], tokens.shape[1] // NC
    others = lax.dynamic_slice(tokens, (0, (1 - core) * half), (count, half))
    theirs = swap(jnp.concatenate([others, out_grad], axis=1))
    rows = lax.ppermute(scaled_rows(w_values, w_scales), tuple(AXES), moves)

    partial = partials(place, tokens, out_grad, theirs)
    rows = gather(rows, FAR)
    total = reduce(partial, NEAR).astype(BF16)
    weights = gather(rows, NEAR)
    total = reduce(total, FAR)
    weight_grad = lax.ppermute(
        total * (1.0 / math.sqrt(count * devices(AXES))), tuple(AXES), [(b, a) for a, b in moves]
    )

    for_them, part, columns = forward(place, tokens, out_grad, theirs, weights)
    projected, token_grad = assemble(place, part, columns, swap(for_them))
    return projected, token_grad, weight_grad


def solution(mesh):
    split = Mesh(mesh.devices.reshape(list(AXES.values())), tuple(AXES))
    by_rows = P(tuple(AXES), None)
    return jax.shard_map(
        body,
        mesh=split,
        in_specs=(by_rows, by_rows, P(), by_rows),
        out_specs=(by_rows, by_rows, by_rows),
        check_vma=False,
    )
```

```python
import math

import jax
import jax.numpy as jnp
from jax import lax
from jax.experimental import pallas as pl
from jax.experimental.pallas import tpu as pltpu
from jax.sharding import Mesh, PartitionSpec as P

BLOCK_ROWS = 4
NZ, NY, NX, NC = 12, 8, 4, 2
AXES = ("z", "y", "x", "c")
BF16 = jnp.bfloat16
F32 = jnp.float32
LONG = 10**11
PARAMS = pltpu.CompilerParams(vmem_limit_bytes=24 * 2**20)


def block_moves():
    moves = []
    for block in range(NZ * NY * NX * NC):
        rest, z = divmod(block, NZ)
        rest, y = divmod(rest, NY)
        c, x = divmod(rest, NX)
        moves.append((block, ((z * NY + y) * NX + x) * NC + c))
    return moves


def scaled_rows(w_values, w_scales):
    rows = w_values.shape[0]
    first = lax.axis_index(AXES) * rows
    start = first // BLOCK_ROWS
    pair = lax.dynamic_slice(w_scales, (start,), (2,))
    block = (first + lax.iota(jnp.int32, rows)) // BLOCK_ROWS - start
    scale = jnp.where(block == 0, pair[0], pair[1])
    return (w_values.astype(F32) * scale[:, None]).astype(BF16)


def swap(array):
    return lax.ppermute(array, "c", [(0, 1), (1, 0)])


def along_x(array, step):
    return lax.ppermute(array, "x", [(i, (i + step) % NX) for i in range(NX)])


def gather(rows, axis, size):
    out = lax.all_to_all(jnp.broadcast_to(rows[None], (size, *rows.shape)), axis, 0, 0)
    return out.reshape(-1, rows.shape[1])


def reduce(rows, axis, size):
    out = lax.all_to_all(rows.reshape(size, -1, rows.shape[1]), axis, 0, 0)
    return jnp.sum(out.astype(F32), axis=0)


def dot(a, b, over):
    return lax.dot_general(a, b, ((over[:1], over[1:]), ((), ())), preferred_element_type=F32)


def whole(shape):
    return pl.BlockSpec(shape, lambda i, place: (0,) * len(shape))


def call(kernel, outs, in_specs, scratch, flops, args):
    moved = sum(math.prod(s.shape) * s.dtype.itemsize for s in outs)
    return pl.pallas_call(
        kernel,
        out_shape=outs,
        grid_spec=pltpu.PrefetchScalarGridSpec(
            num_scalar_prefetch=1,
            grid=(1,),
            in_specs=in_specs,
            out_specs=[whole(s.shape) for s in outs],
            scratch_shapes=scratch,
        ),
        compiler_params=PARAMS,
        cost_estimate=pl.CostEstimate(flops=flops, bytes_accessed=2 * moved, transcendentals=0),
    )(*args)


def partials(place, tokens, grad, theirs):
    count, half = tokens.shape[0], tokens.shape[1] // NC
    cols = grad.shape[1]
    rows = half // NX
    chunk = 256

    def kernel(place_ref, tokens_ref, grad_ref, theirs_ref, *rest):
        outs, total = rest[:NX], rest[NX]
        grads = jnp.concatenate([grad_ref[...], theirs_ref[:, half:]], axis=0)
        for k in range(0, half, chunk):
            both = jnp.concatenate(
                [tokens_ref[:, k : k + chunk], theirs_ref[:, k : k + chunk]], axis=0
            )
            total[k : k + chunk] = dot(both, grads, (0, 0)).astype(BF16)
        x = place_ref[1]
        for step in range(NX):
            block = lax.rem(x + step, NX)
            outs[step][...] = total[pl.ds(pl.multiple_of(block * rows, rows), rows), :]

    return call(
        kernel,
        [jax.ShapeDtypeStruct((rows, cols), BF16)] * NX,
        [
            pl.BlockSpec((count, half), lambda i, place: (0, place[0])),
            whole(grad.shape),
            whole(theirs.shape),
        ],
        [pltpu.VMEM((half, cols), BF16)],
        4 * count * half * cols,
        (place, tokens, grad, theirs),
    )


def forward(place, tokens, grad, theirs, blocks):
    rows, cols = blocks[0].shape
    half = rows * NX
    count = tokens.shape[0]

    def kernel(place_ref, tokens_ref, grad_ref, theirs_ref, *rest):
        block_refs, (for_them, part_ref, columns_ref, weights) = rest[:NX], rest[NX:]
        x = place_ref[1]
        for step in range(NX):
            block = lax.rem(x + NX - step, NX)
            weights[pl.ds(pl.multiple_of(block * rows, rows), rows), :] = block_refs[step][...]
        tokens_both = jnp.concatenate([theirs_ref[:, :half], tokens_ref[...]], axis=0)
        part = dot(tokens_both, weights[...], (1, 0))
        for_them[:, half:] = part[:count].astype(BF16)
        part_ref[...] = part[count:]
        grads = jnp.concatenate([theirs_ref[:, half:], grad_ref[...]], axis=0)
        columns = dot(grads, weights[...], (1, 1)).astype(BF16)
        for_them[:, :half] = columns[:count]
        columns_ref[...] = columns[count:]

    return call(
        kernel,
        [
            jax.ShapeDtypeStruct((count, half + cols), BF16),
            jax.ShapeDtypeStruct((count, cols), F32),
            jax.ShapeDtypeStruct((count, half), BF16),
        ],
        [
            pl.BlockSpec((count, half), lambda i, place: (0, place[0])),
            whole(grad.shape),
            whole(theirs.shape),
            *[whole(b.shape) for b in blocks],
        ],
        [pltpu.VMEM((half, cols), BF16)],
        8 * count * half * cols,
        (place, tokens, grad, theirs, *blocks),
    )


def add_up(place, parts):
    def kernel(place_ref, *refs):
        *part_refs, out_ref = refs
        out_ref[...] = sum(p[...].astype(F32) for p in part_refs).astype(BF16)

    out = jax.ShapeDtypeStruct(parts[0].shape, BF16)
    return call(kernel, [out], [whole(p.shape) for p in parts], [], LONG, (place, *parts))[0]


def assemble(place, part, columns, received):
    count, half = columns.shape
    cols = part.shape[1]

    def kernel(place_ref, part_ref, columns_ref, received_ref, projected_ref, out_ref):
        projected_ref[...] = (part_ref[...] + received_ref[:, half:].astype(F32)).astype(BF16)
        core = place_ref[0]

        @pl.when(core == 0)
        def _():
            out_ref[:, :half] = columns_ref[...]
            out_ref[:, half:] = received_ref[:, :half]

        @pl.when(core == 1)
        def _():
            out_ref[:, :half] = received_ref[:, :half]
            out_ref[:, half:] = columns_ref[...]

    return call(
        kernel,
        [
            jax.ShapeDtypeStruct((count, cols), BF16),
            jax.ShapeDtypeStruct((count, NC * half), BF16),
        ],
        [whole(part.shape), whole(columns.shape), whole(received.shape)],
        [],
        count * cols,
        (place, part, columns, received),
    )


def body(tokens, w_values, w_scales, out_grad):
    moves = block_moves()
    core, x = lax.axis_index("c"), lax.axis_index("x")
    place = jnp.stack([core, x]).astype(jnp.int32)
    half = tokens.shape[1] // NC
    cols = out_grad.shape[1]
    others = lax.dynamic_slice(tokens, (0, (1 - core) * half), (tokens.shape[0], half))
    theirs = swap(jnp.concatenate([others, out_grad], axis=1))
    rows = lax.ppermute(scaled_rows(w_values, w_scales), AXES, moves)

    parts = partials(place, tokens, out_grad, theirs)
    rows, *parts = lax.optimization_barrier((rows, *parts))
    parts = [parts[0], *(along_x(parts[step], step) for step in range(1, NX))]

    rows = gather(gather(rows, "z", NZ), "y", NY)
    total = add_up(place, parts)
    total, rows = lax.optimization_barrier((total, rows))
    blocks = [rows, *(along_x(rows, step) for step in range(1, NX))]

    total = reduce(total, "y", NY).astype(BF16)
    for_them, part, columns = forward(place, tokens, out_grad, theirs, blocks)
    total, for_them = lax.optimization_barrier((total, for_them))
    received = swap(for_them)
    total = reduce(total, "z", NZ)
    count = tokens.shape[0] * NZ * NY * NX * NC
    weight_grad = lax.ppermute(
        total * (1.0 / math.sqrt(count)), AXES, [(b, a) for a, b in moves]
    )
    projected, token_grad = assemble(place, part, columns, received)
    return projected, token_grad, weight_grad


def solution(mesh):
    split = Mesh(mesh.devices.reshape(NZ, NY, NX, NC), AXES)
    by_rows = P(AXES, None)
    return jax.shard_map(
        body,
        mesh=split,
        in_specs=(by_rows, by_rows, P(), by_rows),
        out_specs=(by_rows, by_rows, by_rows),
        check_vma=False,
    )
```

```python
import math

import jax
import jax.numpy as jnp
from jax import lax
from jax.experimental import pallas as pl
from jax.experimental.pallas import tpu as pltpu
from jax.sharding import Mesh, PartitionSpec as P

BLOCK_ROWS = 4
NZ, NY, NX, NC = 12, 8, 4, 2
AXES = ("z", "y", "x", "c")
BF16 = jnp.bfloat16
F32 = jnp.float32
LONG = 10**11
PARAMS = pltpu.CompilerParams(vmem_limit_bytes=24 * 2**20)


def block_moves():
    moves = []
    for block in range(NZ * NY * NX * NC):
        rest, z = divmod(block, NZ)
        rest, y = divmod(rest, NY)
        c, x = divmod(rest, NX)
        moves.append((block, ((z * NY + y) * NX + x) * NC + c))
    return moves


def scaled_rows(w_values, w_scales):
    rows = w_values.shape[0]
    first = lax.axis_index(AXES) * rows
    start = first // BLOCK_ROWS
    pair = lax.dynamic_slice(w_scales, (start,), (2,))
    block = (first + lax.iota(jnp.int32, rows)) // BLOCK_ROWS - start
    scale = jnp.where(block == 0, pair[0], pair[1])
    return (w_values.astype(F32) * scale[:, None]).astype(BF16)


def swap(array):
    return lax.ppermute(array, "c", [(0, 1), (1, 0)])


def along_x(array, step):
    return lax.ppermute(array, "x", [(i, (i + step) % NX) for i in range(NX)])


def gather(rows, axis, size):
    out = lax.all_to_all(jnp.broadcast_to(rows[None], (size, *rows.shape)), axis, 0, 0)
    return out.reshape(-1, rows.shape[1])


def reduce(rows, axis, size):
    out = lax.all_to_all(rows.reshape(size, -1, rows.shape[1]), axis, 0, 0)
    return jnp.sum(out.astype(F32), axis=0)


def dot(a, b, over):
    return lax.dot_general(a, b, ((over[:1], over[1:]), ((), ())), preferred_element_type=F32)


def whole(shape):
    return pl.BlockSpec(shape, lambda i, place: (0,) * len(shape))


def call(kernel, outs, in_specs, scratch, flops, args):
    moved = sum(math.prod(s.shape) * s.dtype.itemsize for s in outs)
    return pl.pallas_call(
        kernel,
        out_shape=outs,
        grid_spec=pltpu.PrefetchScalarGridSpec(
            num_scalar_prefetch=1,
            grid=(1,),
            in_specs=in_specs,
            out_specs=[whole(s.shape) for s in outs],
            scratch_shapes=scratch,
        ),
        compiler_params=PARAMS,
        cost_estimate=pl.CostEstimate(flops=flops, bytes_accessed=2 * moved, transcendentals=0),
    )(*args)


def partials(place, tokens, grad, theirs):
    count, half = tokens.shape[0], tokens.shape[1] // NC
    cols = grad.shape[1]
    rows = half // NX
    chunk = 256

    def kernel(place_ref, tokens_ref, grad_ref, theirs_ref, *rest):
        outs, total = rest[:NX], rest[NX]
        grads = jnp.concatenate([grad_ref[...], theirs_ref[:, half:]], axis=0)
        for k in range(0, half, chunk):
            both = jnp.concatenate(
                [tokens_ref[:, k : k + chunk], theirs_ref[:, k : k + chunk]], axis=0
            )
            total[k : k + chunk] = dot(both, grads, (0, 0)).astype(BF16)
        x = place_ref[1]
        for step in range(NX):
            block = lax.rem(x + step, NX)
            outs[step][...] = total[pl.ds(pl.multiple_of(block * rows, rows), rows), :]

    return call(
        kernel,
        [jax.ShapeDtypeStruct((rows, cols), BF16)] * NX,
        [
            pl.BlockSpec((count, half), lambda i, place: (0, place[0])),
            whole(grad.shape),
            whole(theirs.shape),
        ],
        [pltpu.VMEM((half, cols), BF16)],
        4 * count * half * cols,
        (place, tokens, grad, theirs),
    )


def forward(place, tokens, grad, theirs, blocks):
    rows, cols = blocks[0].shape
    half = rows * NX
    count = tokens.shape[0]

    def kernel(place_ref, tokens_ref, grad_ref, theirs_ref, *rest):
        block_refs, (for_them, part_ref, columns_ref, weights) = rest[:NX], rest[NX:]
        x = place_ref[1]
        for step in range(NX):
            block = lax.rem(x + NX - step, NX)
            weights[pl.ds(pl.multiple_of(block * rows, rows), rows), :] = block_refs[step][...]
        tokens_both = jnp.concatenate([theirs_ref[:, :half], tokens_ref[...]], axis=0)
        part = dot(tokens_both, weights[...], (1, 0))
        for_them[:, half:] = part[:count].astype(BF16)
        part_ref[...] = part[count:]
        grads = jnp.concatenate([theirs_ref[:, half:], grad_ref[...]], axis=0)
        columns = dot(grads, weights[...], (1, 1)).astype(BF16)
        for_them[:, :half] = columns[:count]
        columns_ref[...] = columns[count:]

    return call(
        kernel,
        [
            jax.ShapeDtypeStruct((count, half + cols), BF16),
            jax.ShapeDtypeStruct((count, cols), F32),
            jax.ShapeDtypeStruct((count, half), BF16),
        ],
        [
            pl.BlockSpec((count, half), lambda i, place: (0, place[0])),
            whole(grad.shape),
            whole(theirs.shape),
            *[whole(b.shape) for b in blocks],
        ],
        [pltpu.VMEM((half, cols), BF16)],
        8 * count * half * cols,
        (place, tokens, grad, theirs, *blocks),
    )


def add_up(place, parts):
    def kernel(place_ref, *refs):
        *part_refs, out_ref = refs
        out_ref[...] = sum(p[...].astype(F32) for p in part_refs).astype(BF16)

    out = jax.ShapeDtypeStruct(parts[0].shape, BF16)
    return call(kernel, [out], [whole(p.shape) for p in parts], [], LONG, (place, *parts))[0]


def assemble(place, part, columns, received):
    count, half = columns.shape
    cols = part.shape[1]

    def kernel(place_ref, part_ref, columns_ref, received_ref, projected_ref, out_ref):
        projected_ref[...] = (part_ref[...] + received_ref[:, half:].astype(F32)).astype(BF16)
        core = place_ref[0]

        @pl.when(core == 0)
        def _():
            out_ref[:, :half] = columns_ref[...]
            out_ref[:, half:] = received_ref[:, :half]

        @pl.when(core == 1)
        def _():
            out_ref[:, :half] = received_ref[:, :half]
            out_ref[:, half:] = columns_ref[...]

    return call(
        kernel,
        [
            jax.ShapeDtypeStruct((count, cols), BF16),
            jax.ShapeDtypeStruct((count, NC * half), BF16),
        ],
        [whole(part.shape), whole(columns.shape), whole(received.shape)],
        [],
        count * cols,
        (place, part, columns, received),
    )


def body(tokens, w_values, w_scales, out_grad):
    moves = block_moves()
    core, x = lax.axis_index("c"), lax.axis_index("x")
    place = jnp.stack([core, x]).astype(jnp.int32)
    half = tokens.shape[1] // NC
    cols = out_grad.shape[1]
    others = lax.dynamic_slice(tokens, (0, (1 - core) * half), (tokens.shape[0], half))
    theirs = swap(jnp.concatenate([others, out_grad], axis=1))
    rows = lax.ppermute(scaled_rows(w_values, w_scales), AXES, moves)

    rows = gather(rows, "z", NZ)
    theirs, rows = lax.optimization_barrier((theirs, rows))

    parts = partials(place, tokens, out_grad, theirs)
    rows, *parts = lax.optimization_barrier((rows, *parts))
    parts = [parts[0], *(along_x(parts[step], step) for step in range(1, NX))]
    rows = gather(rows, "y", NY)
    total = add_up(place, parts)
    total, rows = lax.optimization_barrier((total, rows))
    blocks = [rows, *(along_x(rows, step) for step in range(1, NX))]

    total = reduce(total, "y", NY).astype(BF16)
    total = reduce(total, "z", NZ)
    total, *blocks = lax.optimization_barrier((total, *blocks))
    count = tokens.shape[0] * NZ * NY * NX * NC
    weight_grad = lax.ppermute(
        total * (1.0 / math.sqrt(count)), AXES, [(b, a) for a, b in moves]
    )
    for_them, part, columns = forward(place, tokens, out_grad, theirs, blocks)
    projected, token_grad = assemble(place, part, columns, swap(for_them))
    return projected, token_grad, weight_grad


def solution(mesh):
    split = Mesh(mesh.devices.reshape(NZ, NY, NX, NC), AXES)
    by_rows = P(AXES, None)
    return jax.shard_map(
        body,
        mesh=split,
        in_specs=(by_rows, by_rows, P(), by_rows),
        out_specs=(by_rows, by_rows, by_rows),
        check_vma=False,
    )
```

```python
import math

import ml_dtypes
import numpy as np
import jax
import jax.numpy as jnp
from jax import lax
from jax.experimental import pallas as pl
from jax.experimental.pallas import tpu as pltpu
from jax.sharding import Mesh, PartitionSpec as P

BLOCK_ROWS = 4
NZ, NY, NX, NC = 12, 8, 4, 2
AXES = ("z", "y", "x", "c")
BF16 = jnp.bfloat16
F32 = jnp.float32
LONG = 10**11
PARAMS = pltpu.CompilerParams(vmem_limit_bytes=24 * 2**20)


PLANES = 2


def column_order(rows):
    size = PLANES * NY * NX * NC * rows
    places = np.arange(size).reshape(PLANES, NY, NX, NC, rows).transpose(3, 2, 0, 1, 4)
    order = np.zeros((size, size), ml_dtypes.bfloat16)
    order[places.reshape(-1), np.arange(size)] = 1
    return order


def scaled_rows(w_values, w_scales):
    rows = w_values.shape[0]
    first = lax.axis_index(AXES) * rows
    start = first // BLOCK_ROWS
    pair = lax.dynamic_slice(w_scales, (start,), (2,))
    block = (first + lax.iota(jnp.int32, rows)) // BLOCK_ROWS - start
    scale = jnp.where(block == 0, pair[0], pair[1])
    return (w_values.astype(F32) * scale[:, None]).astype(BF16)


def swap(array):
    return lax.ppermute(array, "c", [(0, 1), (1, 0)])


def along_x(array, step):
    return lax.ppermute(array, "x", [(i, (i + step) % NX) for i in range(NX)])


def gather(rows, axis, size):
    out = lax.all_to_all(jnp.broadcast_to(rows[None], (size, *rows.shape)), axis, 0, 0)
    return out.reshape(-1, rows.shape[1])


def reduce(rows, axis, size):
    out = lax.all_to_all(rows.reshape(size, -1, rows.shape[1]), axis, 0, 0)
    return jnp.sum(out.astype(F32), axis=0)


def dot(a, b, over):
    return lax.dot_general(a, b, ((over[:1], over[1:]), ((), ())), preferred_element_type=F32)


def whole(shape):
    return pl.BlockSpec(shape, lambda i, place: (0,) * len(shape))


def call(kernel, outs, in_specs, scratch, flops, args):
    moved = sum(math.prod(s.shape) * s.dtype.itemsize for s in outs)
    return pl.pallas_call(
        kernel,
        out_shape=outs,
        grid_spec=pltpu.PrefetchScalarGridSpec(
            num_scalar_prefetch=1,
            grid=(1,),
            in_specs=in_specs,
            out_specs=[whole(s.shape) for s in outs],
            scratch_shapes=scratch,
        ),
        compiler_params=PARAMS,
        cost_estimate=pl.CostEstimate(flops=flops, bytes_accessed=2 * moved, transcendentals=0),
    )(*args)


def sort_columns(place, tokens, grad, order):
    count, cols = grad.shape
    half = tokens.shape[1] // NC
    window = order.shape[0]
    part = window // NC

    def kernel(place_ref, tokens_ref, grad_ref, order_ref, mine_ref, send_ref):
        first = place_ref[0] == 0
        for k in range(tokens.shape[1] // window):
            both = dot(tokens_ref[:, k * window : (k + 1) * window], order_ref[...], (1, 0))
            low, high = both[:, :part], both[:, part:]
            at = slice(k * part, (k + 1) * part)
            mine_ref[:, at] = jnp.where(first, low, high).astype(BF16)
            send_ref[:, at] = jnp.where(first, high, low).astype(BF16)
        send_ref[:, half:] = grad_ref[...]

    return call(
        kernel,
        [
            jax.ShapeDtypeStruct((count, half), BF16),
            jax.ShapeDtypeStruct((count, half + cols), BF16),
        ],
        [whole(tokens.shape), whole(grad.shape), whole(order.shape)],
        [],
        2 * tokens.size * window,
        (place, tokens, grad, order),
    )


def x_rows(window, block, part):
    return pl.multiple_of(window * part * NX + block * part, part)


def partials(place, mine, grad, theirs, part):
    count, half = mine.shape
    cols = grad.shape[1]
    rows = half // NX
    chunk = 256

    def kernel(place_ref, mine_ref, grad_ref, theirs_ref, *rest):
        outs, total = rest[:NX], rest[NX]
        grads = jnp.concatenate([grad_ref[...], theirs_ref[:, half:]], axis=0)
        for k in range(0, half, chunk):
            both = jnp.concatenate(
                [mine_ref[:, k : k + chunk], theirs_ref[:, k : k + chunk]], axis=0
            )
            total[k : k + chunk] = dot(both, grads, (0, 0)).astype(BF16)
        x = place_ref[1]
        for step in range(NX):
            block = lax.rem(x + step, NX)
            for k in range(rows // part):
                outs[step][k * part : (k + 1) * part] = total[
                    pl.ds(x_rows(k, block, part), part), :
                ]

    return call(
        kernel,
        [jax.ShapeDtypeStruct((rows, cols), BF16)] * NX,
        [whole(mine.shape), whole(grad.shape), whole(theirs.shape)],
        [pltpu.VMEM((half, cols), BF16)],
        4 * count * half * cols,
        (place, mine, grad, theirs),
    )


def forward(place, mine, grad, theirs, blocks, part_rows):
    rows, cols = blocks[0].shape
    half = rows * NX
    count = mine.shape[0]

    def kernel(place_ref, mine_ref, grad_ref, theirs_ref, *rest):
        block_refs, (for_them, part_ref, columns_ref, weights) = rest[:NX], rest[NX:]
        x = place_ref[1]
        for step in range(NX):
            block = lax.rem(x + NX - step, NX)
            for k in range(rows // part_rows):
                weights[pl.ds(x_rows(k, block, part_rows), part_rows), :] = block_refs[step][
                    k * part_rows : (k + 1) * part_rows
                ]
        tokens_both = jnp.concatenate([theirs_ref[:, :half], mine_ref[...]], axis=0)
        part = dot(tokens_both, weights[...], (1, 0))
        for_them[:, half:] = part[:count].astype(BF16)
        part_ref[...] = part[count:]
        grads = jnp.concatenate([theirs_ref[:, half:], grad_ref[...]], axis=0)
        columns = dot(grads, weights[...], (1, 1)).astype(BF16)
        for_them[:, :half] = columns[:count]
        columns_ref[...] = columns[count:]

    return call(
        kernel,
        [
            jax.ShapeDtypeStruct((count, half + cols), BF16),
            jax.ShapeDtypeStruct((count, cols), F32),
            jax.ShapeDtypeStruct((count, half), BF16),
        ],
        [
            whole(mine.shape),
            whole(grad.shape),
            whole(theirs.shape),
            *[whole(b.shape) for b in blocks],
        ],
        [pltpu.VMEM((half, cols), BF16)],
        8 * count * half * cols,
        (place, mine, grad, theirs, *blocks),
    )


def add_up(place, parts):
    def kernel(place_ref, *refs):
        *part_refs, out_ref = refs
        out_ref[...] = sum(p[...].astype(F32) for p in part_refs).astype(BF16)

    out = jax.ShapeDtypeStruct(parts[0].shape, BF16)
    return call(kernel, [out], [whole(p.shape) for p in parts], [], LONG, (place, *parts))[0]


def assemble(place, part, columns, received, order):
    count, half = columns.shape
    cols = part.shape[1]
    window = order.shape[0]
    width = window // NC

    def kernel(place_ref, part_ref, columns_ref, received_ref, order_ref, projected_ref, out_ref):
        projected_ref[...] = (part_ref[...] + received_ref[:, half:].astype(F32)).astype(BF16)

        def put(low_ref, high_ref):
            for k in range(half // width):
                at = slice(k * width, (k + 1) * width)
                both = jnp.concatenate([low_ref[:, at], high_ref[:, at]], axis=1)
                out_ref[:, k * window : (k + 1) * window] = dot(
                    both, order_ref[...], (1, 1)
                ).astype(BF16)

        @pl.when(place_ref[0] == 0)
        def _():
            put(columns_ref, received_ref)

        @pl.when(place_ref[0] == 1)
        def _():
            put(received_ref, columns_ref)

    return call(
        kernel,
        [
            jax.ShapeDtypeStruct((count, cols), BF16),
            jax.ShapeDtypeStruct((count, NC * half), BF16),
        ],
        [whole(part.shape), whole(columns.shape), whole(received.shape), whole(order.shape)],
        [],
        2 * NC * count * half * window,
        (place, part, columns, received, order),
    )


def body(tokens, w_values, w_scales, out_grad):
    core, x = lax.axis_index("c"), lax.axis_index("x")
    place = jnp.stack([core, x]).astype(jnp.int32)
    order = jnp.asarray(column_order(w_values.shape[0]))
    part_rows = order.shape[0] // (NC * NX)
    mine, send = sort_columns(place, tokens, out_grad, order)
    theirs = swap(send)
    rows = gather(scaled_rows(w_values, w_scales), "y", NY)
    theirs, rows = lax.optimization_barrier((theirs, rows))

    parts = partials(place, mine, out_grad, theirs, part_rows)
    rows, *parts = lax.optimization_barrier((rows, *parts))
    parts = [parts[0], *(along_x(parts[step], step) for step in range(1, NX))]
    rows = gather(rows, "z", NZ)
    total = add_up(place, parts)
    total, rows = lax.optimization_barrier((total, rows))
    blocks = [rows, *(along_x(rows, step) for step in range(1, NX))]

    total = reduce(total, "z", NZ).astype(BF16)
    total = reduce(total, "y", NY)
    total, *blocks = lax.optimization_barrier((total, *blocks))
    count = tokens.shape[0] * NZ * NY * NX * NC
    weight_grad = total * (1.0 / math.sqrt(count))
    for_them, part, columns = forward(place, mine, out_grad, theirs, blocks, part_rows)
    projected, token_grad = assemble(place, part, columns, swap(for_them), order)
    return projected, token_grad, weight_grad


def solution(mesh):
    split = Mesh(mesh.devices.reshape(NZ, NY, NX, NC), AXES)
    by_rows = P(AXES, None)
    return jax.shard_map(
        body,
        mesh=split,
        in_specs=(by_rows, by_rows, P(), by_rows),
        out_specs=(by_rows, by_rows, by_rows),
        check_vma=False,
    )
```

```python
import math

import ml_dtypes
import numpy as np
import jax
import jax.numpy as jnp
from jax import lax
from jax.experimental import pallas as pl
from jax.experimental.pallas import tpu as pltpu
from jax.sharding import Mesh, PartitionSpec as P

BLOCK_ROWS = 4
NZ, NY, NX, NC = 12, 8, 4, 2
AXES = ("z", "y", "x", "c")
BF16 = jnp.bfloat16
F32 = jnp.float32
LONG = 10**11
PARAMS = pltpu.CompilerParams(vmem_limit_bytes=24 * 2**20)


PLANES = 2


def column_order(rows):
    size = PLANES * NY * NX * NC * rows
    places = np.arange(size).reshape(PLANES, NY, NX, NC, rows).transpose(3, 2, 0, 1, 4)
    order = np.zeros((size, size), ml_dtypes.bfloat16)
    order[places.reshape(-1), np.arange(size)] = 1
    return order


def scaled_rows(w_values, w_scales):
    rows = w_values.shape[0]
    first = lax.axis_index(AXES) * rows
    start = first // BLOCK_ROWS
    pair = lax.dynamic_slice(w_scales, (start,), (2,))
    block = (first + lax.iota(jnp.int32, rows)) // BLOCK_ROWS - start
    scale = jnp.where(block == 0, pair[0], pair[1])
    return (w_values.astype(F32) * scale[:, None]).astype(BF16)


def swap(array):
    return lax.ppermute(array, "c", [(0, 1), (1, 0)])


def along_x(array, step):
    return lax.ppermute(array, "x", [(i, (i + step) % NX) for i in range(NX)])


def gather(rows, axis, size):
    out = lax.all_to_all(jnp.broadcast_to(rows[None], (size, *rows.shape)), axis, 0, 0)
    return out.reshape(-1, rows.shape[1])


def reduce(rows, axis, size):
    out = lax.all_to_all(rows.reshape(size, -1, rows.shape[1]), axis, 0, 0)
    return jnp.sum(out.astype(F32), axis=0)


def dot(a, b, over):
    return lax.dot_general(a, b, ((over[:1], over[1:]), ((), ())), preferred_element_type=F32)


def whole(shape):
    return pl.BlockSpec(shape, lambda i, place: (0,) * len(shape))


def call(kernel, outs, in_specs, scratch, flops, args):
    moved = sum(math.prod(s.shape) * s.dtype.itemsize for s in outs)
    return pl.pallas_call(
        kernel,
        out_shape=outs,
        grid_spec=pltpu.PrefetchScalarGridSpec(
            num_scalar_prefetch=1,
            grid=(1,),
            in_specs=in_specs,
            out_specs=[whole(s.shape) for s in outs],
            scratch_shapes=scratch,
        ),
        compiler_params=PARAMS,
        cost_estimate=pl.CostEstimate(flops=flops, bytes_accessed=2 * moved, transcendentals=0),
    )(*args)


def sort_columns(place, tokens, grad, order):
    count, cols = grad.shape
    half = tokens.shape[1] // NC
    window = order.shape[0]
    part = window // NC

    def kernel(place_ref, tokens_ref, grad_ref, order_ref, mine_ref, send_ref):
        first = place_ref[0] == 0
        for k in range(tokens.shape[1] // window):
            both = dot(tokens_ref[:, k * window : (k + 1) * window], order_ref[...], (1, 0))
            low, high = both[:, :part], both[:, part:]
            at = slice(k * part, (k + 1) * part)
            mine_ref[:, at] = jnp.where(first, low, high).astype(BF16)
            send_ref[:, at] = jnp.where(first, high, low).astype(BF16)
        send_ref[:, half:] = grad_ref[...]

    return call(
        kernel,
        [
            jax.ShapeDtypeStruct((count, half), BF16),
            jax.ShapeDtypeStruct((count, half + cols), BF16),
        ],
        [whole(tokens.shape), whole(grad.shape), whole(order.shape)],
        [],
        2 * tokens.size * window,
        (place, tokens, grad, order),
    )


def x_rows(window, block, part):
    return pl.multiple_of(window * part * NX + block * part, part)


def partials(place, mine, grad, theirs, part):
    count, half = mine.shape
    cols = grad.shape[1]
    rows = half // NX
    chunk = 256

    def kernel(place_ref, mine_ref, grad_ref, theirs_ref, *rest):
        outs, total = rest[:NX], rest[NX]
        grads = jnp.concatenate([grad_ref[...], theirs_ref[:, half:]], axis=0)
        for k in range(0, half, chunk):
            both = jnp.concatenate(
                [mine_ref[:, k : k + chunk], theirs_ref[:, k : k + chunk]], axis=0
            )
            total[k : k + chunk] = dot(both, grads, (0, 0)).astype(BF16)
        x = place_ref[1]
        for step in range(NX):
            block = lax.rem(x + step, NX)
            for k in range(rows // part):
                outs[step][k * part : (k + 1) * part] = total[
                    pl.ds(x_rows(k, block, part), part), :
                ]

    return call(
        kernel,
        [jax.ShapeDtypeStruct((rows, cols), BF16)] * NX,
        [whole(mine.shape), whole(grad.shape), whole(theirs.shape)],
        [pltpu.VMEM((half, cols), BF16)],
        4 * count * half * cols,
        (place, mine, grad, theirs),
    )


def forward(place, mine, grad, theirs, blocks, part_rows):
    rows, cols = blocks[0].shape
    half = rows * NX
    count = mine.shape[0]

    def kernel(place_ref, mine_ref, grad_ref, theirs_ref, *rest):
        block_refs, (for_them, part_ref, columns_ref, weights) = rest[:NX], rest[NX:]
        x = place_ref[1]
        for step in range(NX):
            block = lax.rem(x + NX - step, NX)
            for k in range(rows // part_rows):
                weights[pl.ds(x_rows(k, block, part_rows), part_rows), :] = block_refs[step][
                    k * part_rows : (k + 1) * part_rows
                ]
        tokens_both = jnp.concatenate([theirs_ref[:, :half], mine_ref[...]], axis=0)
        part = dot(tokens_both, weights[...], (1, 0))
        for_them[:, half:] = part[:count].astype(BF16)
        part_ref[...] = part[count:]
        grads = jnp.concatenate([theirs_ref[:, half:], grad_ref[...]], axis=0)
        columns = dot(grads, weights[...], (1, 1)).astype(BF16)
        for_them[:, :half] = columns[:count]
        columns_ref[...] = columns[count:]

    return call(
        kernel,
        [
            jax.ShapeDtypeStruct((count, half + cols), BF16),
            jax.ShapeDtypeStruct((count, cols), F32),
            jax.ShapeDtypeStruct((count, half), BF16),
        ],
        [
            whole(mine.shape),
            whole(grad.shape),
            whole(theirs.shape),
            *[whole(b.shape) for b in blocks],
        ],
        [pltpu.VMEM((half, cols), BF16)],
        8 * count * half * cols,
        (place, mine, grad, theirs, *blocks),
    )


def assemble(place, part, columns, received, order):
    count, half = columns.shape
    cols = part.shape[1]
    window = order.shape[0]
    width = window // NC

    def kernel(place_ref, part_ref, columns_ref, received_ref, order_ref, projected_ref, out_ref):
        projected_ref[...] = (part_ref[...] + received_ref[:, half:].astype(F32)).astype(BF16)

        def put(low_ref, high_ref):
            for k in range(half // width):
                at = slice(k * width, (k + 1) * width)
                both = jnp.concatenate([low_ref[:, at], high_ref[:, at]], axis=1)
                out_ref[:, k * window : (k + 1) * window] = dot(
                    both, order_ref[...], (1, 1)
                ).astype(BF16)

        @pl.when(place_ref[0] == 0)
        def _():
            put(columns_ref, received_ref)

        @pl.when(place_ref[0] == 1)
        def _():
            put(received_ref, columns_ref)

    return call(
        kernel,
        [
            jax.ShapeDtypeStruct((count, cols), BF16),
            jax.ShapeDtypeStruct((count, NC * half), BF16),
        ],
        [whole(part.shape), whole(columns.shape), whole(received.shape), whole(order.shape)],
        [],
        LONG,
        (place, part, columns, received, order),
    )


def body(tokens, w_values, w_scales, out_grad):
    core, x = lax.axis_index("c"), lax.axis_index("x")
    place = jnp.stack([core, x]).astype(jnp.int32)
    order = jnp.asarray(column_order(w_values.shape[0]))
    part_rows = order.shape[0] // (NC * NX)
    mine, send = sort_columns(place, tokens, out_grad, order)
    theirs = swap(send)
    rows = gather(scaled_rows(w_values, w_scales), "y", NY)
    theirs, rows = lax.optimization_barrier((theirs, rows))

    parts = partials(place, mine, out_grad, theirs, part_rows)
    rows, *parts = lax.optimization_barrier((rows, *parts))
    parts = [parts[0], *(along_x(parts[step], step) for step in range(1, NX))]
    rows = gather(rows, "z", NZ)
    total = sum(p.astype(F32) for p in parts).astype(BF16)
    total, rows = lax.optimization_barrier((total, rows))
    blocks = [rows, *(along_x(rows, step) for step in range(1, NX))]

    total = reduce(total, "z", NZ).astype(BF16)
    for_them, part, columns = forward(place, mine, out_grad, theirs, blocks, part_rows)
    total, for_them = lax.optimization_barrier((total, for_them))
    received = swap(for_them)
    total = lax.all_to_all(total.reshape(NY, -1, total.shape[1]), "y", 0, 0)
    projected, token_grad = assemble(place, part, columns, received, order)
    total, projected, token_grad = lax.optimization_barrier((total, projected, token_grad))
    total = jnp.sum(total.astype(F32), axis=0)
    count = tokens.shape[0] * NZ * NY * NX * NC
    weight_grad = total * (1.0 / math.sqrt(count))
    return projected, token_grad, weight_grad


def solution(mesh):
    split = Mesh(mesh.devices.reshape(NZ, NY, NX, NC), AXES)
    by_rows = P(AXES, None)
    return jax.shard_map(
        body,
        mesh=split,
        in_specs=(by_rows, by_rows, P(), by_rows),
        out_specs=(by_rows, by_rows, by_rows),
        check_vma=False,
    )
```

```python
import math

import ml_dtypes
import numpy as np
import jax
import jax.numpy as jnp
from jax import lax
from jax.experimental import pallas as pl
from jax.experimental.pallas import tpu as pltpu
from jax.sharding import Mesh, PartitionSpec as P

BLOCK_ROWS = 4
NZ, NY, NX, NC = 12, 8, 4, 2
AXES = ("z", "y", "x", "c")
BF16 = jnp.bfloat16
F32 = jnp.float32
LONG = 10**11
PARAMS = pltpu.CompilerParams(vmem_limit_bytes=24 * 2**20)


PLANES = 2


def column_order(rows):
    size = PLANES * NY * NX * NC * rows
    places = np.arange(size).reshape(PLANES, NY, NX, NC, rows).transpose(3, 2, 0, 1, 4)
    order = np.zeros((size, size), ml_dtypes.bfloat16)
    order[places.reshape(-1), np.arange(size)] = 1
    return order


def swap(array):
    return lax.ppermute(array, "c", [(0, 1), (1, 0)])


def along_x(array, step):
    return lax.ppermute(array, "x", [(i, (i + step) % NX) for i in range(NX)])


def gather(rows, axis, size):
    out = lax.all_to_all(jnp.broadcast_to(rows[None], (size, *rows.shape)), axis, 0, 0)
    return out.reshape(-1, rows.shape[1])


def reduce(rows, axis, size):
    out = lax.all_to_all(rows.reshape(size, -1, rows.shape[1]), axis, 0, 0)
    return jnp.sum(out.astype(F32), axis=0)


def dot(a, b, over):
    return lax.dot_general(a, b, ((over[:1], over[1:]), ((), ())), preferred_element_type=F32)


def whole(shape):
    return pl.BlockSpec(shape, lambda i, place: (0,) * len(shape))


def call(kernel, outs, in_specs, scratch, flops, args):
    moved = sum(math.prod(s.shape) * s.dtype.itemsize for s in outs)
    return pl.pallas_call(
        kernel,
        out_shape=outs,
        grid_spec=pltpu.PrefetchScalarGridSpec(
            num_scalar_prefetch=1,
            grid=(1,),
            in_specs=in_specs,
            out_specs=[whole(s.shape) for s in outs],
            scratch_shapes=scratch,
        ),
        compiler_params=PARAMS,
        cost_estimate=pl.CostEstimate(flops=flops, bytes_accessed=2 * moved, transcendentals=0),
    )(*args)


def sort_columns(place, tokens, grad, order, w_values, w_scales):
    count, cols = grad.shape
    half = tokens.shape[1] // NC
    window = order.shape[0]
    part = window // NC
    windows = tokens.shape[1] // window
    rows = w_values.shape[0]

    def kernel(
        place_ref,
        scales_ref,
        tokens_ref,
        order_ref,
        grad_ref,
        values_ref,
        mine_ref,
        send_ref,
        rows_ref,
        tokens_here,
        order_here,
        sems,
        order_sem,
    ):
        fetch_order = pltpu.make_async_copy(order_ref, order_here, order_sem)
        fetch_order.start()
        fetches = [
            pltpu.make_async_copy(
                tokens_ref.at[:, pl.ds(k * window, window)], tokens_here.at[k], sems.at[k]
            )
            for k in range(windows)
        ]
        for fetch in fetches:
            fetch.start()

        first_row = place_ref[2] * rows
        start = lax.div(first_row, BLOCK_ROWS)
        row = first_row + lax.broadcasted_iota(jnp.int32, (rows, cols), 0)
        scale = jnp.where(
            row < (start + 1) * BLOCK_ROWS, scales_ref[start], scales_ref[start + 1]
        )
        scaled = (values_ref[...].astype(F32) * scale).astype(BF16)
        for k in range(NY):
            rows_ref[k] = scaled
        send_ref[:, half:] = grad_ref[...]

        fetch_order.wait()
        first = place_ref[0] == 0
        for k, fetch in enumerate(fetches):
            fetch.wait()
            both = dot(tokens_here[k], order_here[...], (1, 0))
            low, high = both[:, :part], both[:, part:]
            at = slice(k * part, (k + 1) * part)
            mine_ref[:, at] = jnp.where(first, low, high).astype(BF16)
            send_ref[:, at] = jnp.where(first, high, low).astype(BF16)

    smem = pl.BlockSpec(memory_space=pltpu.SMEM)
    vmem = pl.BlockSpec(memory_space=pltpu.VMEM)
    hbm = pl.BlockSpec(memory_space=pltpu.HBM)
    return pl.pallas_call(
        kernel,
        out_shape=[
            jax.ShapeDtypeStruct((count, half), BF16),
            jax.ShapeDtypeStruct((count, half + cols), BF16),
            jax.ShapeDtypeStruct((NY, rows, cols), BF16),
        ],
        in_specs=[smem, smem, hbm, hbm, vmem, vmem],
        out_specs=[vmem] * 3,
        scratch_shapes=[
            pltpu.VMEM((windows, count, window), BF16),
            pltpu.VMEM(order.shape, BF16),
            pltpu.SemaphoreType.DMA((windows,)),
            pltpu.SemaphoreType.DMA,
        ],
        compiler_params=PARAMS,
        cost_estimate=pl.CostEstimate(
            flops=2 * tokens.size * window, bytes_accessed=6 * tokens.size, transcendentals=0
        ),
    )(place, w_scales, tokens, order, grad, w_values)


def x_rows(window, block, part):
    return pl.multiple_of(window * part * NX + block * part, part)


def partials(place, mine, grad, theirs, part):
    count, half = mine.shape
    cols = grad.shape[1]
    rows = half // NX
    chunk = 256

    def kernel(place_ref, mine_ref, grad_ref, theirs_ref, *rest):
        outs, total = rest[:NX], rest[NX]
        grads = jnp.concatenate([grad_ref[...], theirs_ref[:, half:]], axis=0)
        for k in range(0, half, chunk):
            both = jnp.concatenate(
                [mine_ref[:, k : k + chunk], theirs_ref[:, k : k + chunk]], axis=0
            )
            total[k : k + chunk] = dot(both, grads, (0, 0)).astype(BF16)
        x = place_ref[1]
        for step in range(NX):
            block = lax.rem(x + step, NX)
            for k in range(rows // part):
                outs[step][k * part : (k + 1) * part] = total[
                    pl.ds(x_rows(k, block, part), part), :
                ]

    return call(
        kernel,
        [jax.ShapeDtypeStruct((rows, cols), BF16)] * NX,
        [whole(mine.shape), whole(grad.shape), whole(theirs.shape)],
        [pltpu.VMEM((half, cols), BF16)],
        4 * count * half * cols,
        (place, mine, grad, theirs),
    )


def forward(place, mine, grad, theirs, blocks, part_rows):
    rows, cols = blocks[0].shape
    half = rows * NX
    count = mine.shape[0]

    def kernel(place_ref, mine_ref, grad_ref, theirs_ref, *rest):
        block_refs, (for_them, part_ref, columns_ref, weights) = rest[:NX], rest[NX:]
        x = place_ref[1]
        for step in range(NX):
            block = lax.rem(x + NX - step, NX)
            for k in range(rows // part_rows):
                weights[pl.ds(x_rows(k, block, part_rows), part_rows), :] = block_refs[step][
                    k * part_rows : (k + 1) * part_rows
                ]
        tokens_both = jnp.concatenate([theirs_ref[:, :half], mine_ref[...]], axis=0)
        part = dot(tokens_both, weights[...], (1, 0))
        for_them[:, half:] = part[:count].astype(BF16)
        part_ref[...] = part[count:]
        grads = jnp.concatenate([theirs_ref[:, half:], grad_ref[...]], axis=0)
        columns = dot(grads, weights[...], (1, 1)).astype(BF16)
        for_them[:, :half] = columns[:count]
        columns_ref[...] = columns[count:]

    return call(
        kernel,
        [
            jax.ShapeDtypeStruct((count, half + cols), BF16),
            jax.ShapeDtypeStruct((count, cols), F32),
            jax.ShapeDtypeStruct((count, half), BF16),
        ],
        [
            whole(mine.shape),
            whole(grad.shape),
            whole(theirs.shape),
            *[whole(b.shape) for b in blocks],
        ],
        [pltpu.VMEM((half, cols), BF16)],
        8 * count * half * cols,
        (place, mine, grad, theirs, *blocks),
    )


def add_up(place, parts):
    def kernel(place_ref, *refs):
        *part_refs, out_ref = refs
        out_ref[...] = sum(p[...].astype(F32) for p in part_refs).astype(BF16)

    out = jax.ShapeDtypeStruct(parts[0].shape, BF16)
    return call(kernel, [out], [whole(p.shape) for p in parts], [], LONG, (place, *parts))[0]


def assemble(place, part, columns, received, order):
    count, half = columns.shape
    cols = part.shape[1]
    window = order.shape[0]
    width = window // NC
    windows = half // width

    def kernel(
        place_ref,
        part_ref,
        columns_ref,
        received_ref,
        order_ref,
        projected_ref,
        out_ref,
        out_here,
        sems,
    ):
        def leave(k):
            return pltpu.make_async_copy(
                out_here.at[k], out_ref.at[:, pl.ds(k * window, window)], sems.at[k]
            )

        first = place_ref[0] == 0
        for k in range(windows):
            at = slice(k * width, (k + 1) * width)
            own, other = columns_ref[:, at].astype(F32), received_ref[:, at].astype(F32)
            both = jnp.concatenate(
                [jnp.where(first, own, other), jnp.where(first, other, own)], axis=1
            )
            out_here[k] = dot(both.astype(BF16), order_ref[...], (1, 1)).astype(BF16)
            leave(k).start()
        projected_ref[...] = (part_ref[...] + received_ref[:, half:].astype(F32)).astype(BF16)
        for k in range(windows):
            leave(k).wait()

    vmem = pl.BlockSpec(memory_space=pltpu.VMEM)
    return pl.pallas_call(
        kernel,
        out_shape=[
            jax.ShapeDtypeStruct((count, cols), BF16),
            jax.ShapeDtypeStruct((count, NC * half), BF16),
        ],
        in_specs=[pl.BlockSpec(memory_space=pltpu.SMEM), *[vmem] * 4],
        out_specs=[vmem, pl.BlockSpec(memory_space=pltpu.HBM)],
        scratch_shapes=[
            pltpu.VMEM((windows, count, window), BF16),
            pltpu.SemaphoreType.DMA((windows,)),
        ],
        compiler_params=PARAMS,
        cost_estimate=pl.CostEstimate(
            flops=2 * NC * count * half * window,
            bytes_accessed=8 * count * half,
            transcendentals=0,
        ),
    )(place, part, columns, received, order)


def body(tokens, w_values, w_scales, out_grad):
    core, x = lax.axis_index("c"), lax.axis_index("x")
    place = jnp.stack([core, x, lax.axis_index(AXES)]).astype(jnp.int32)
    order = jnp.asarray(column_order(w_values.shape[0]))
    part_rows = order.shape[0] // (NC * NX)
    mine, send, rows = sort_columns(place, tokens, out_grad, order, w_values, w_scales)
    theirs = swap(send)
    rows = lax.all_to_all(rows, "y", 0, 0).reshape(-1, out_grad.shape[1])
    theirs, rows = lax.optimization_barrier((theirs, rows))

    parts = partials(place, mine, out_grad, theirs, part_rows)
    rows, *parts = lax.optimization_barrier((rows, *parts))
    parts = [parts[0], *(along_x(parts[step], step) for step in range(1, NX))]
    rows = gather(rows, "z", NZ)
    total = add_up(place, parts)
    total, rows = lax.optimization_barrier((total, rows))
    blocks = [rows, *(along_x(rows, step) for step in range(1, NX))]

    total = reduce(total, "z", NZ).astype(BF16)
    total = reduce(total, "y", NY)
    total, *blocks = lax.optimization_barrier((total, *blocks))
    count = tokens.shape[0] * NZ * NY * NX * NC
    weight_grad = total * (1.0 / math.sqrt(count))
    for_them, part, columns = forward(place, mine, out_grad, theirs, blocks, part_rows)
    projected, token_grad = assemble(place, part, columns, swap(for_them), order)
    return projected, token_grad, weight_grad


def solution(mesh):
    split = Mesh(mesh.devices.reshape(NZ, NY, NX, NC), AXES)
    by_rows = P(AXES, None)
    return jax.shard_map(
        body,
        mesh=split,
        in_specs=(by_rows, by_rows, P(), by_rows),
        out_specs=(by_rows, by_rows, by_rows),
        check_vma=False,
    )
```

```python
import math

import ml_dtypes
import numpy as np
import jax
import jax.numpy as jnp
from jax import lax
from jax.experimental import pallas as pl
from jax.experimental.pallas import tpu as pltpu
from jax.sharding import Mesh, PartitionSpec as P

BLOCK_ROWS = 4
NZ, NY, NX, NC = 12, 8, 4, 2
AXES = ("z", "y", "x", "c")
BF16 = jnp.bfloat16
F32 = jnp.float32
LONG = 10**11
PARAMS = pltpu.CompilerParams(vmem_limit_bytes=24 * 2**20)


PLANES = 2


def column_order(rows):
    size = PLANES * NY * NX * NC * rows
    places = np.arange(size).reshape(PLANES, NY, NX, NC, rows).transpose(3, 2, 0, 1, 4)
    order = np.zeros((size, size), ml_dtypes.bfloat16)
    order[places.reshape(-1), np.arange(size)] = 1
    return order


def swap(array):
    return lax.ppermute(array, "c", [(0, 1), (1, 0)])


def along_x(array, step):
    return lax.ppermute(array, "x", [(i, (i + step) % NX) for i in range(NX)])


def gather(rows, axis, size):
    out = lax.all_to_all(jnp.broadcast_to(rows[None], (size, *rows.shape)), axis, 0, 0)
    return out.reshape(-1, rows.shape[1])


def reduce(rows, axis, size):
    out = lax.all_to_all(rows.reshape(size, -1, rows.shape[1]), axis, 0, 0)
    return jnp.sum(out.astype(F32), axis=0)


def dot(a, b, over):
    return lax.dot_general(a, b, ((over[:1], over[1:]), ((), ())), preferred_element_type=F32)


def whole(shape):
    return pl.BlockSpec(shape, lambda i, place: (0,) * len(shape))


def call(kernel, outs, in_specs, scratch, flops, args):
    moved = sum(math.prod(s.shape) * s.dtype.itemsize for s in outs)
    return pl.pallas_call(
        kernel,
        out_shape=outs,
        grid_spec=pltpu.PrefetchScalarGridSpec(
            num_scalar_prefetch=1,
            grid=(1,),
            in_specs=in_specs,
            out_specs=[whole(s.shape) for s in outs],
            scratch_shapes=scratch,
        ),
        compiler_params=PARAMS,
        cost_estimate=pl.CostEstimate(flops=flops, bytes_accessed=2 * moved, transcendentals=0),
    )(*args)


def sort_columns(place, tokens, grad, order, w_values, w_scales):
    count, cols = grad.shape
    half = tokens.shape[1] // NC
    window = order.shape[0]
    part = window // NC
    windows = tokens.shape[1] // window
    rows = w_values.shape[0]

    def kernel(
        place_ref,
        scales_ref,
        tokens_ref,
        order_ref,
        grad_ref,
        values_ref,
        mine_ref,
        send_ref,
        rows_ref,
    ):
        first_row = place_ref[2] * rows
        start = lax.div(first_row, BLOCK_ROWS)
        row = first_row + lax.broadcasted_iota(jnp.int32, (rows, cols), 0)
        scale = jnp.where(
            row < (start + 1) * BLOCK_ROWS, scales_ref[start], scales_ref[start + 1]
        )
        scaled = (values_ref[...].astype(F32) * scale).astype(BF16)
        for k in range(NY):
            rows_ref[k] = scaled
        send_ref[:, half:] = grad_ref[...]

        stacked = jnp.concatenate(
            [tokens_ref[:, k * window : (k + 1) * window] for k in range(windows)], axis=0
        )
        for core, out_ref in ((place_ref[0], mine_ref), (1 - place_ref[0], send_ref)):
            columns = order_ref[:, pl.ds(pl.multiple_of(core * part, part), part)]
            chosen = dot(stacked, columns, (1, 0)).astype(BF16)
            for k in range(windows):
                out_ref[:, k * part : (k + 1) * part] = chosen[k * count : (k + 1) * count]

    smem = pl.BlockSpec(memory_space=pltpu.SMEM)
    vmem = pl.BlockSpec(memory_space=pltpu.VMEM)
    return pl.pallas_call(
        kernel,
        out_shape=[
            jax.ShapeDtypeStruct((count, half), BF16),
            jax.ShapeDtypeStruct((count, half + cols), BF16),
            jax.ShapeDtypeStruct((NY, rows, cols), BF16),
        ],
        in_specs=[smem, smem, *[vmem] * 4],
        out_specs=[vmem] * 3,
        compiler_params=PARAMS,
        cost_estimate=pl.CostEstimate(
            flops=2 * tokens.size * window, bytes_accessed=6 * tokens.size, transcendentals=0
        ),
    )(place, w_scales, tokens, order, grad, w_values)


def x_rows(window, block, part):
    return pl.multiple_of(window * part * NX + block * part, part)


def partials(place, mine, grad, theirs, part):
    count, half = mine.shape
    cols = grad.shape[1]
    rows = half // NX
    chunk = 256

    def kernel(place_ref, mine_ref, grad_ref, theirs_ref, *rest):
        outs, total = rest[:NX], rest[NX]
        grads = jnp.concatenate([grad_ref[...], theirs_ref[:, half:]], axis=0)
        for k in range(0, half, chunk):
            both = jnp.concatenate(
                [mine_ref[:, k : k + chunk], theirs_ref[:, k : k + chunk]], axis=0
            )
            total[k : k + chunk] = dot(both, grads, (0, 0)).astype(BF16)
        x = place_ref[1]
        for step in range(NX):
            block = lax.rem(x + step, NX)
            for k in range(rows // part):
                outs[step][k * part : (k + 1) * part] = total[
                    pl.ds(x_rows(k, block, part), part), :
                ]

    return call(
        kernel,
        [jax.ShapeDtypeStruct((rows, cols), BF16)] * NX,
        [whole(mine.shape), whole(grad.shape), whole(theirs.shape)],
        [pltpu.VMEM((half, cols), BF16)],
        4 * count * half * cols,
        (place, mine, grad, theirs),
    )


def forward(place, mine, grad, theirs, blocks, part_rows):
    rows, cols = blocks[0].shape
    half = rows * NX
    count = mine.shape[0]

    def kernel(place_ref, mine_ref, grad_ref, theirs_ref, *rest):
        block_refs, (for_them, part_ref, columns_ref, weights) = rest[:NX], rest[NX:]
        x = place_ref[1]
        for step in range(NX):
            block = lax.rem(x + NX - step, NX)
            for k in range(rows // part_rows):
                weights[pl.ds(x_rows(k, block, part_rows), part_rows), :] = block_refs[step][
                    k * part_rows : (k + 1) * part_rows
                ]
        tokens_both = jnp.concatenate([theirs_ref[:, :half], mine_ref[...]], axis=0)
        part = dot(tokens_both, weights[...], (1, 0))
        for_them[:, half:] = part[:count].astype(BF16)
        part_ref[...] = part[count:]
        grads = jnp.concatenate([theirs_ref[:, half:], grad_ref[...]], axis=0)
        columns = dot(grads, weights[...], (1, 1)).astype(BF16)
        for_them[:, :half] = columns[:count]
        columns_ref[...] = columns[count:]

    return call(
        kernel,
        [
            jax.ShapeDtypeStruct((count, half + cols), BF16),
            jax.ShapeDtypeStruct((count, cols), F32),
            jax.ShapeDtypeStruct((count, half), BF16),
        ],
        [
            whole(mine.shape),
            whole(grad.shape),
            whole(theirs.shape),
            *[whole(b.shape) for b in blocks],
        ],
        [pltpu.VMEM((half, cols), BF16)],
        8 * count * half * cols,
        (place, mine, grad, theirs, *blocks),
    )


def add_up(place, parts):
    def kernel(place_ref, *refs):
        *part_refs, out_ref = refs
        out_ref[...] = sum(p[...].astype(F32) for p in part_refs).astype(BF16)

    out = jax.ShapeDtypeStruct(parts[0].shape, BF16)
    return call(kernel, [out], [whole(p.shape) for p in parts], [], LONG, (place, *parts))[0]


def assemble(place, part, columns, received, order):
    count, half = columns.shape
    cols = part.shape[1]
    window = order.shape[0]
    width = window // NC
    windows = half // width

    def kernel(
        place_ref,
        part_ref,
        columns_ref,
        received_ref,
        order_ref,
        projected_ref,
        out_ref,
        out_here,
        sems,
    ):
        def leave(k):
            return pltpu.make_async_copy(
                out_here.at[k], out_ref.at[:, pl.ds(k * window, window)], sems.at[k]
            )

        total = None
        for core, side_ref in ((place_ref[0], columns_ref), (1 - place_ref[0], received_ref)):
            stacked = jnp.concatenate(
                [side_ref[:, k * width : (k + 1) * width] for k in range(windows)], axis=0
            )
            order_half = order_ref[:, pl.ds(pl.multiple_of(core * width, width), width)]
            product = dot(stacked, order_half, (1, 1))
            total = product if total is None else total + product
        for k in range(windows):
            out_here[k] = total[k * count : (k + 1) * count].astype(BF16)
            leave(k).start()
        projected_ref[...] = (part_ref[...] + received_ref[:, half:].astype(F32)).astype(BF16)
        for k in range(windows):
            leave(k).wait()

    vmem = pl.BlockSpec(memory_space=pltpu.VMEM)
    return pl.pallas_call(
        kernel,
        out_shape=[
            jax.ShapeDtypeStruct((count, cols), BF16),
            jax.ShapeDtypeStruct((count, NC * half), BF16),
        ],
        in_specs=[pl.BlockSpec(memory_space=pltpu.SMEM), *[vmem] * 4],
        out_specs=[vmem, pl.BlockSpec(memory_space=pltpu.HBM)],
        scratch_shapes=[
            pltpu.VMEM((windows, count, window), BF16),
            pltpu.SemaphoreType.DMA((windows,)),
        ],
        compiler_params=PARAMS,
        cost_estimate=pl.CostEstimate(
            flops=2 * NC * count * half * window,
            bytes_accessed=8 * count * half,
            transcendentals=0,
        ),
    )(place, part, columns, received, order)


def body(tokens, w_values, w_scales, out_grad):
    core, x = lax.axis_index("c"), lax.axis_index("x")
    place = jnp.stack([core, x, lax.axis_index(AXES)]).astype(jnp.int32)
    order = jnp.asarray(column_order(w_values.shape[0]))
    part_rows = order.shape[0] // (NC * NX)
    mine, send, rows = sort_columns(place, tokens, out_grad, order, w_values, w_scales)
    theirs = swap(send)
    rows = lax.all_to_all(rows, "y", 0, 0).reshape(-1, out_grad.shape[1])
    theirs, rows = lax.optimization_barrier((theirs, rows))

    parts = partials(place, mine, out_grad, theirs, part_rows)
    rows, *parts = lax.optimization_barrier((rows, *parts))
    parts = [parts[0], *(along_x(parts[step], step) for step in range(1, NX))]
    rows = gather(rows, "z", NZ)
    total = add_up(place, parts)
    total, rows = lax.optimization_barrier((total, rows))
    blocks = [rows, *(along_x(rows, step) for step in range(1, NX))]

    total = reduce(total, "z", NZ).astype(BF16)
    total = reduce(total, "y", NY)
    total, *blocks = lax.optimization_barrier((total, *blocks))
    count = tokens.shape[0] * NZ * NY * NX * NC
    weight_grad = total * (1.0 / math.sqrt(count))
    for_them, part, columns = forward(place, mine, out_grad, theirs, blocks, part_rows)
    projected, token_grad = assemble(place, part, columns, swap(for_them), order)
    return projected, token_grad, weight_grad


def solution(mesh):
    split = Mesh(mesh.devices.reshape(NZ, NY, NX, NC), AXES)
    by_rows = P(AXES, None)
    return jax.shard_map(
        body,
        mesh=split,
        in_specs=(by_rows, by_rows, P(), by_rows),
        out_specs=(by_rows, by_rows, by_rows),
        check_vma=False,
    )
```

```python
import math

import ml_dtypes
import numpy as np
import jax
import jax.numpy as jnp
from jax import lax
from jax.experimental import pallas as pl
from jax.experimental.pallas import tpu as pltpu
from jax.sharding import Mesh, PartitionSpec as P

BLOCK_ROWS = 4
NZ, NY, NX, NC = 12, 8, 4, 2
AXES = ("z", "y", "x", "c")
BF16 = jnp.bfloat16
F32 = jnp.float32
LONG = 10**11
PARAMS = pltpu.CompilerParams(vmem_limit_bytes=24 * 2**20)


PLANES = 2


def column_order(rows):
    size = PLANES * NY * NX * NC * rows
    places = np.arange(size).reshape(PLANES, NY, NX, NC, rows).transpose(3, 2, 0, 1, 4)
    order = np.zeros((size, size), ml_dtypes.bfloat16)
    order[places.reshape(-1), np.arange(size)] = 1
    return order


def swap(array):
    return lax.ppermute(array, "c", [(0, 1), (1, 0)])


def along_x(array, step):
    return lax.ppermute(array, "x", [(i, (i + step) % NX) for i in range(NX)])


def gather(rows, axis, size):
    out = lax.all_to_all(jnp.broadcast_to(rows[None], (size, *rows.shape)), axis, 0, 0)
    return out.reshape(-1, rows.shape[1])


def reduce(rows, axis, size):
    out = lax.all_to_all(rows.reshape(size, -1, rows.shape[1]), axis, 0, 0)
    return jnp.sum(out.astype(F32), axis=0)


def dot(a, b, over):
    return lax.dot_general(a, b, ((over[:1], over[1:]), ((), ())), preferred_element_type=F32)


def whole(shape):
    return pl.BlockSpec(shape, lambda i, place: (0,) * len(shape))


def call(kernel, outs, in_specs, scratch, flops, args):
    moved = sum(math.prod(s.shape) * s.dtype.itemsize for s in outs)
    return pl.pallas_call(
        kernel,
        out_shape=outs,
        grid_spec=pltpu.PrefetchScalarGridSpec(
            num_scalar_prefetch=1,
            grid=(1,),
            in_specs=in_specs,
            out_specs=[whole(s.shape) for s in outs],
            scratch_shapes=scratch,
        ),
        compiler_params=PARAMS,
        cost_estimate=pl.CostEstimate(flops=flops, bytes_accessed=2 * moved, transcendentals=0),
    )(*args)


def sort_columns(place, tokens, grad, order, w_values, w_scales):
    count, cols = grad.shape
    half = tokens.shape[1] // NC
    window = order.shape[0]
    part = window // NC
    windows = tokens.shape[1] // window
    rows = w_values.shape[0]

    def kernel(
        place_ref,
        scales_ref,
        tokens_ref,
        order_ref,
        grad_ref,
        values_ref,
        mine_ref,
        send_ref,
        rows_ref,
        tokens_here,
        order_here,
        sems,
        order_sem,
    ):
        fetches = [pltpu.make_async_copy(order_ref, order_here, order_sem)]
        for k in range(windows):
            at = pl.ds(k * window, window)
            fetches.append(
                pltpu.make_async_copy(tokens_ref.at[:, at], tokens_here.at[k], sems.at[k])
            )
        for fetch in fetches:
            fetch.start()

        first_row = place_ref[2] * rows
        start = lax.div(first_row, BLOCK_ROWS)
        row = first_row + lax.broadcasted_iota(jnp.int32, (rows, cols), 0)
        scale = jnp.where(
            row < (start + 1) * BLOCK_ROWS, scales_ref[start], scales_ref[start + 1]
        )
        scaled = (values_ref[...].astype(F32) * scale).astype(BF16)
        for k in range(NY):
            rows_ref[k] = scaled
        send_ref[:, half:] = grad_ref[...]

        for fetch in fetches:
            fetch.wait()
        stacked = tokens_here[...].reshape(windows * count, window)
        for core, out_ref in ((place_ref[0], mine_ref), (1 - place_ref[0], send_ref)):
            columns = order_here[:, pl.ds(pl.multiple_of(core * part, part), part)]
            chosen = dot(stacked, columns, (1, 0)).astype(BF16)
            for k in range(windows):
                out_ref[:, k * part : (k + 1) * part] = chosen[k * count : (k + 1) * count]

    smem = pl.BlockSpec(memory_space=pltpu.SMEM)
    hbm = pl.BlockSpec(memory_space=pltpu.HBM)
    vmem = pl.BlockSpec(memory_space=pltpu.VMEM)
    return pl.pallas_call(
        kernel,
        out_shape=[
            jax.ShapeDtypeStruct((count, half), BF16),
            jax.ShapeDtypeStruct((count, half + cols), BF16),
            jax.ShapeDtypeStruct((NY, rows, cols), BF16),
        ],
        in_specs=[smem, smem, hbm, hbm, vmem, vmem],
        out_specs=[vmem] * 3,
        scratch_shapes=[
            pltpu.VMEM((windows, count, window), BF16),
            pltpu.VMEM(order.shape, BF16),
            pltpu.SemaphoreType.DMA((windows,)),
            pltpu.SemaphoreType.DMA,
        ],
        compiler_params=pltpu.CompilerParams(vmem_limit_bytes=56 * 2**20),
        cost_estimate=pl.CostEstimate(
            flops=2 * tokens.size * window, bytes_accessed=6 * tokens.size, transcendentals=0
        ),
    )(place, w_scales, tokens, order, grad, w_values)


def x_rows(window, block, part):
    return pl.multiple_of(window * part * NX + block * part, part)


def partials(place, mine, grad, theirs, part):
    count, half = mine.shape
    cols = grad.shape[1]
    rows = half // NX
    chunk = 256

    def kernel(place_ref, mine_ref, grad_ref, theirs_ref, *rest):
        outs, total = rest[:NX], rest[NX]
        grads = jnp.concatenate([grad_ref[...], theirs_ref[:, half:]], axis=0)
        for k in range(0, half, chunk):
            both = jnp.concatenate(
                [mine_ref[:, k : k + chunk], theirs_ref[:, k : k + chunk]], axis=0
            )
            total[k : k + chunk] = dot(both, grads, (0, 0)).astype(BF16)
        x = place_ref[1]
        for step in range(NX):
            block = lax.rem(x + step, NX)
            for k in range(rows // part):
                outs[step][k * part : (k + 1) * part] = total[
                    pl.ds(x_rows(k, block, part), part), :
                ]

    return call(
        kernel,
        [jax.ShapeDtypeStruct((rows, cols), BF16)] * NX,
        [whole(mine.shape), whole(grad.shape), whole(theirs.shape)],
        [pltpu.VMEM((half, cols), BF16)],
        4 * count * half * cols,
        (place, mine, grad, theirs),
    )


def forward(place, mine, grad, theirs, blocks, part_rows):
    rows, cols = blocks[0].shape
    half = rows * NX
    count = mine.shape[0]

    def kernel(place_ref, mine_ref, grad_ref, theirs_ref, *rest):
        block_refs, (for_them, part_ref, columns_ref, weights) = rest[:NX], rest[NX:]
        x = place_ref[1]
        for step in range(NX):
            block = lax.rem(x + NX - step, NX)
            for k in range(rows // part_rows):
                weights[pl.ds(x_rows(k, block, part_rows), part_rows), :] = block_refs[step][
                    k * part_rows : (k + 1) * part_rows
                ]
        tokens_both = jnp.concatenate([theirs_ref[:, :half], mine_ref[...]], axis=0)
        part = dot(tokens_both, weights[...], (1, 0))
        for_them[:, half:] = part[:count].astype(BF16)
        part_ref[...] = part[count:]
        grads = jnp.concatenate([theirs_ref[:, half:], grad_ref[...]], axis=0)
        columns = dot(grads, weights[...], (1, 1)).astype(BF16)
        for_them[:, :half] = columns[:count]
        columns_ref[...] = columns[count:]

    return call(
        kernel,
        [
            jax.ShapeDtypeStruct((count, half + cols), BF16),
            jax.ShapeDtypeStruct((count, cols), F32),
            jax.ShapeDtypeStruct((count, half), BF16),
        ],
        [
            whole(mine.shape),
            whole(grad.shape),
            whole(theirs.shape),
            *[whole(b.shape) for b in blocks],
        ],
        [pltpu.VMEM((half, cols), BF16)],
        8 * count * half * cols,
        (place, mine, grad, theirs, *blocks),
    )


def add_up(place, parts):
    def kernel(place_ref, *refs):
        *part_refs, out_ref = refs
        out_ref[...] = sum(p[...].astype(F32) for p in part_refs).astype(BF16)

    out = jax.ShapeDtypeStruct(parts[0].shape, BF16)
    return call(kernel, [out], [whole(p.shape) for p in parts], [], LONG, (place, *parts))[0]


def assemble(place, part, columns, received, order):
    count, half = columns.shape
    cols = part.shape[1]
    window = order.shape[0]
    width = window // NC
    windows = half // width

    def kernel(
        place_ref,
        part_ref,
        columns_ref,
        received_ref,
        order_ref,
        projected_ref,
        out_ref,
        out_here,
        sems,
    ):
        def leave(k):
            return pltpu.make_async_copy(
                out_here.at[k], out_ref.at[:, pl.ds(k * window, window)], sems.at[k]
            )

        total = None
        for core, side_ref in ((place_ref[0], columns_ref), (1 - place_ref[0], received_ref)):
            stacked = jnp.concatenate(
                [side_ref[:, k * width : (k + 1) * width] for k in range(windows)], axis=0
            )
            order_half = order_ref[:, pl.ds(pl.multiple_of(core * width, width), width)]
            product = dot(stacked, order_half, (1, 1))
            total = product if total is None else total + product
        for k in range(windows):
            out_here[k] = total[k * count : (k + 1) * count].astype(BF16)
            leave(k).start()
        projected_ref[...] = (part_ref[...] + received_ref[:, half:].astype(F32)).astype(BF16)
        for k in range(windows):
            leave(k).wait()

    vmem = pl.BlockSpec(memory_space=pltpu.VMEM)
    return pl.pallas_call(
        kernel,
        out_shape=[
            jax.ShapeDtypeStruct((count, cols), BF16),
            jax.ShapeDtypeStruct((count, NC * half), BF16),
        ],
        in_specs=[pl.BlockSpec(memory_space=pltpu.SMEM), *[vmem] * 4],
        out_specs=[vmem, pl.BlockSpec(memory_space=pltpu.HBM)],
        scratch_shapes=[
            pltpu.VMEM((windows, count, window), BF16),
            pltpu.SemaphoreType.DMA((windows,)),
        ],
        compiler_params=PARAMS,
        cost_estimate=pl.CostEstimate(
            flops=2 * NC * count * half * window,
            bytes_accessed=8 * count * half,
            transcendentals=0,
        ),
    )(place, part, columns, received, order)


def body(tokens, w_values, w_scales, out_grad):
    core, x = lax.axis_index("c"), lax.axis_index("x")
    place = jnp.stack([core, x, lax.axis_index(AXES)]).astype(jnp.int32)
    order = jnp.asarray(column_order(w_values.shape[0]))
    part_rows = order.shape[0] // (NC * NX)
    mine, send, rows = sort_columns(place, tokens, out_grad, order, w_values, w_scales)
    theirs = swap(send)
    rows = lax.all_to_all(rows, "y", 0, 0).reshape(-1, out_grad.shape[1])
    theirs, rows = lax.optimization_barrier((theirs, rows))

    parts = partials(place, mine, out_grad, theirs, part_rows)
    rows, *parts = lax.optimization_barrier((rows, *parts))
    parts = [parts[0], *(along_x(parts[step], step) for step in range(1, NX))]
    rows = gather(rows, "z", NZ)
    total = add_up(place, parts)
    total, rows = lax.optimization_barrier((total, rows))
    blocks = [rows, *(along_x(rows, step) for step in range(1, NX))]

    total = reduce(total, "z", NZ).astype(BF16)
    total = reduce(total, "y", NY)
    total, *blocks = lax.optimization_barrier((total, *blocks))
    count = tokens.shape[0] * NZ * NY * NX * NC
    weight_grad = total * (1.0 / math.sqrt(count))
    for_them, part, columns = forward(place, mine, out_grad, theirs, blocks, part_rows)
    projected, token_grad = assemble(place, part, columns, swap(for_them), order)
    return projected, token_grad, weight_grad


def solution(mesh):
    split = Mesh(mesh.devices.reshape(NZ, NY, NX, NC), AXES)
    by_rows = P(AXES, None)
    return jax.shard_map(
        body,
        mesh=split,
        in_specs=(by_rows, by_rows, P(), by_rows),
        out_specs=(by_rows, by_rows, by_rows),
        check_vma=False,
    )
```

```python
import math

import ml_dtypes
import numpy as np
import jax
import jax.numpy as jnp
from jax import lax
from jax.experimental import pallas as pl
from jax.experimental.pallas import tpu as pltpu
from jax.sharding import Mesh, PartitionSpec as P

BLOCK_ROWS = 4
NZ, NY, NX, NC = 12, 8, 4, 2
AXES = ("z", "y", "x", "c")
BF16 = jnp.bfloat16
F32 = jnp.float32
PARAMS = pltpu.CompilerParams(vmem_limit_bytes=24 * 2**20)


PLANES = 2


def column_order(rows):
    size = PLANES * NY * NX * NC * rows
    places = np.arange(size).reshape(PLANES, NY, NX, NC, rows).transpose(3, 2, 0, 1, 4)
    order = np.zeros((size, size), ml_dtypes.bfloat16)
    order[places.reshape(-1), np.arange(size)] = 1
    return order


def swap(array):
    return lax.ppermute(array, "c", [(0, 1), (1, 0)])


def along_x(array, step):
    return lax.ppermute(array, "x", [(i, (i + step) % NX) for i in range(NX)])


def gather(rows, axis, size):
    out = lax.all_to_all(jnp.broadcast_to(rows[None], (size, *rows.shape)), axis, 0, 0)
    return out.reshape(-1, rows.shape[1])


def reduce(rows, axis, size):
    out = lax.all_to_all(rows.reshape(size, -1, rows.shape[1]), axis, 0, 0)
    return jnp.sum(out.astype(F32), axis=0)


def dot(a, b, over):
    return lax.dot_general(a, b, ((over[:1], over[1:]), ((), ())), preferred_element_type=F32)


def whole(shape):
    return pl.BlockSpec(shape, lambda i, place: (0,) * len(shape))


def call(kernel, outs, in_specs, scratch, flops, args):
    moved = sum(math.prod(s.shape) * s.dtype.itemsize for s in outs)
    return pl.pallas_call(
        kernel,
        out_shape=outs,
        grid_spec=pltpu.PrefetchScalarGridSpec(
            num_scalar_prefetch=1,
            grid=(1,),
            in_specs=in_specs,
            out_specs=[whole(s.shape) for s in outs],
            scratch_shapes=scratch,
        ),
        compiler_params=PARAMS,
        cost_estimate=pl.CostEstimate(flops=flops, bytes_accessed=2 * moved, transcendentals=0),
    )(*args)


def sort_columns(place, tokens, grad, order, w_values, w_scales):
    count, cols = grad.shape
    half = tokens.shape[1] // NC
    window = order.shape[0]
    part = window // NC
    windows = tokens.shape[1] // window
    rows = w_values.shape[0]

    def kernel(
        place_ref,
        scales_ref,
        tokens_ref,
        order_ref,
        grad_ref,
        values_ref,
        mine_ref,
        send_ref,
        rows_ref,
    ):
        first_row = place_ref[2] * rows
        start = lax.div(first_row, BLOCK_ROWS)
        row = first_row + lax.broadcasted_iota(jnp.int32, (rows, cols), 0)
        scale = jnp.where(
            row < (start + 1) * BLOCK_ROWS, scales_ref[start], scales_ref[start + 1]
        )
        scaled = (values_ref[...].astype(F32) * scale).astype(BF16)
        for k in range(NY):
            rows_ref[k] = scaled
        send_ref[:, half:] = grad_ref[...]

        stacked = jnp.concatenate(
            [tokens_ref[:, k * window : (k + 1) * window] for k in range(windows)], axis=0
        )
        for core, out_ref in ((place_ref[0], mine_ref), (1 - place_ref[0], send_ref)):
            columns = order_ref[:, pl.ds(pl.multiple_of(core * part, part), part)]
            chosen = dot(stacked, columns, (1, 0)).astype(BF16)
            for k in range(windows):
                out_ref[:, k * part : (k + 1) * part] = chosen[k * count : (k + 1) * count]

    smem = pl.BlockSpec(memory_space=pltpu.SMEM)
    vmem = pl.BlockSpec(memory_space=pltpu.VMEM)
    return pl.pallas_call(
        kernel,
        out_shape=[
            jax.ShapeDtypeStruct((count, half), BF16),
            jax.ShapeDtypeStruct((count, half + cols), BF16),
            jax.ShapeDtypeStruct((NY, rows, cols), BF16),
        ],
        in_specs=[smem, smem, *[vmem] * 4],
        out_specs=[vmem] * 3,
        compiler_params=PARAMS,
        cost_estimate=pl.CostEstimate(
            flops=2 * tokens.size * window, bytes_accessed=6 * tokens.size, transcendentals=0
        ),
    )(place, w_scales, tokens, order, grad, w_values)


def x_rows(window, block, part):
    return pl.multiple_of(window * part * NX + block * part, part)


def partials(place, mine, grad, theirs, part):
    count, half = mine.shape
    cols = grad.shape[1]
    rows = half // NX
    chunk = 256

    def kernel(place_ref, mine_ref, grad_ref, theirs_ref, *rest):
        outs, total = rest[:NX], rest[NX]
        grads = jnp.concatenate([grad_ref[...], theirs_ref[:, half:]], axis=0)
        for k in range(0, half, chunk):
            both = jnp.concatenate(
                [mine_ref[:, k : k + chunk], theirs_ref[:, k : k + chunk]], axis=0
            )
            total[k : k + chunk] = dot(both, grads, (0, 0)).astype(BF16)
        x = place_ref[1]
        for step in range(NX):
            block = lax.rem(x + step, NX)
            for k in range(rows // part):
                outs[step][k * part : (k + 1) * part] = total[
                    pl.ds(x_rows(k, block, part), part), :
                ]

    return call(
        kernel,
        [jax.ShapeDtypeStruct((rows, cols), BF16)] * NX,
        [whole(mine.shape), whole(grad.shape), whole(theirs.shape)],
        [pltpu.VMEM((half, cols), BF16)],
        4 * count * half * cols,
        (place, mine, grad, theirs),
    )


def forward(place, mine, grad, theirs, blocks, part_rows):
    rows, cols = blocks[0].shape
    half = rows * NX
    count = mine.shape[0]

    def kernel(place_ref, mine_ref, grad_ref, theirs_ref, *rest):
        block_refs, (for_them, part_ref, columns_ref, weights) = rest[:NX], rest[NX:]
        x = place_ref[1]
        for step in range(NX):
            block = lax.rem(x + NX - step, NX)
            for k in range(rows // part_rows):
                weights[pl.ds(x_rows(k, block, part_rows), part_rows), :] = block_refs[step][
                    k * part_rows : (k + 1) * part_rows
                ]
        tokens_both = jnp.concatenate([theirs_ref[:, :half], mine_ref[...]], axis=0)
        part = dot(tokens_both, weights[...], (1, 0))
        for_them[:, half:] = part[:count].astype(BF16)
        part_ref[...] = part[count:]
        grads = jnp.concatenate([theirs_ref[:, half:], grad_ref[...]], axis=0)
        columns = dot(grads, weights[...], (1, 1)).astype(BF16)
        for_them[:, :half] = columns[:count]
        columns_ref[...] = columns[count:]

    return call(
        kernel,
        [
            jax.ShapeDtypeStruct((count, half + cols), BF16),
            jax.ShapeDtypeStruct((count, cols), F32),
            jax.ShapeDtypeStruct((count, half), BF16),
        ],
        [
            whole(mine.shape),
            whole(grad.shape),
            whole(theirs.shape),
            *[whole(b.shape) for b in blocks],
        ],
        [pltpu.VMEM((half, cols), BF16)],
        8 * count * half * cols,
        (place, mine, grad, theirs, *blocks),
    )


def assemble(place, part, columns, received, order):
    count, half = columns.shape
    cols = part.shape[1]
    window = order.shape[0]
    width = window // NC
    windows = half // width

    def kernel(
        place_ref,
        part_ref,
        columns_ref,
        received_ref,
        order_ref,
        projected_ref,
        out_ref,
        out_here,
        sems,
    ):
        def leave(k):
            return pltpu.make_async_copy(
                out_here.at[k], out_ref.at[:, pl.ds(k * window, window)], sems.at[k]
            )

        total = None
        for core, side_ref in ((place_ref[0], columns_ref), (1 - place_ref[0], received_ref)):
            stacked = jnp.concatenate(
                [side_ref[:, k * width : (k + 1) * width] for k in range(windows)], axis=0
            )
            order_half = order_ref[:, pl.ds(pl.multiple_of(core * width, width), width)]
            product = dot(stacked, order_half, (1, 1))
            total = product if total is None else total + product
        for k in range(windows):
            out_here[k] = total[k * count : (k + 1) * count].astype(BF16)
            leave(k).start()
        projected_ref[...] = (part_ref[...] + received_ref[:, half:].astype(F32)).astype(BF16)
        for k in range(windows):
            leave(k).wait()

    vmem = pl.BlockSpec(memory_space=pltpu.VMEM)
    return pl.pallas_call(
        kernel,
        out_shape=[
            jax.ShapeDtypeStruct((count, cols), BF16),
            jax.ShapeDtypeStruct((count, NC * half), BF16),
        ],
        in_specs=[pl.BlockSpec(memory_space=pltpu.SMEM), *[vmem] * 4],
        out_specs=[vmem, pl.BlockSpec(memory_space=pltpu.HBM)],
        scratch_shapes=[
            pltpu.VMEM((windows, count, window), BF16),
            pltpu.SemaphoreType.DMA((windows,)),
        ],
        compiler_params=PARAMS,
        cost_estimate=pl.CostEstimate(
            flops=2 * NC * count * half * window,
            bytes_accessed=8 * count * half,
            transcendentals=0,
        ),
    )(place, part, columns, received, order)


def body(tokens, w_values, w_scales, out_grad):
    core, x = lax.axis_index("c"), lax.axis_index("x")
    place = jnp.stack([core, x, lax.axis_index(AXES)]).astype(jnp.int32)
    order = jnp.asarray(column_order(w_values.shape[0]))
    part_rows = order.shape[0] // (NC * NX)
    mine, send, rows = sort_columns(place, tokens, out_grad, order, w_values, w_scales)
    theirs = swap(send)
    rows = lax.all_to_all(rows, "y", 0, 0).reshape(-1, out_grad.shape[1])
    theirs, rows = lax.optimization_barrier((theirs, rows))

    parts = partials(place, mine, out_grad, theirs, part_rows)
    rows, *parts = lax.optimization_barrier((rows, *parts))
    parts = [parts[0], *(along_x(parts[step], step) for step in range(1, NX))]
    rows = gather(rows, "z", NZ)
    total = sum(p.astype(F32) for p in parts).astype(BF16)
    total, rows = lax.optimization_barrier((total, rows))
    blocks = [rows, *(along_x(rows, step) for step in range(1, NX))]

    total = reduce(total, "z", NZ).astype(BF16)
    total = reduce(total, "y", NY)
    total, *blocks = lax.optimization_barrier((total, *blocks))
    count = tokens.shape[0] * NZ * NY * NX * NC
    weight_grad = total * (1.0 / math.sqrt(count))
    for_them, part, columns = forward(place, mine, out_grad, theirs, blocks, part_rows)
    projected, token_grad = assemble(place, part, columns, swap(for_them), order)
    return projected, token_grad, weight_grad


def solution(mesh):
    split = Mesh(mesh.devices.reshape(NZ, NY, NX, NC), AXES)
    by_rows = P(AXES, None)
    return jax.shard_map(
        body,
        mesh=split,
        in_specs=(by_rows, by_rows, P(), by_rows),
        out_specs=(by_rows, by_rows, by_rows),
        check_vma=False,
    )
```
